256 devices in a mesh: dp: 4 (over y), ctx: 32 (over x, z), chan: 2 (over core).
Axes of the slice: x: 4, y: 4, z: 8, core: 2. Of those that a mesh axis runs over, the one named last changes fastest.
Arguments:
- inputs: bfloat16 [4, 4096, 2, 2048], P('dp', 'ctx', None, 'chan'), may hold values from -6 to 6
- cotangent: bfloat16 [4, 4096, 2048], P('dp', 'ctx'), may hold values from -6 to 6
- out_proj: bfloat16 [2048, 2, 2048], P('dp', None, 'chan'), may hold values from -0.09375 to 0.09375
- modulus: float32 [2048], P('chan'), may hold values from 0.93 to 1, as said below
- phase: float32 [2048], P('chan'), may hold values from -3.140625 to 3.140625
- gain: float32 [2048], P('chan'), may hold values from 0 to 1, as said below
- retain: float32 [4, 4096], P('dp', 'ctx'), may hold values from 0.5 to 1
- doc_starts: int32 [4, 8], P('dp'), may hold values from 0 to 4095, as said below
- row_blocks: int32 [4], P('dp'), may hold values from 1 to 32, as said below
Outputs:
- grad_inputs: bfloat16 [4, 4096, 2, 2048], P('dp', 'ctx', None, 'chan')
- grad_proj: float32 [2048, 2, 2048], P(('dp', 'ctx'), None, 'chan')
- grad_eigen: float32 [2, 2048], P(None, 'chan')
- grad_gain: float32 [2048], P('chan')
The draws below stay inside these ranges and needn't reach their ends.
Inputs may be any that keep to these rules, and one draw needn't show every extreme that they name: `doc_starts`: the first entry of each row is 0; some row has a document beginning at position 4095. `row_blocks`: one row has all 32 blocks. `modulus`: strictly below 1. `gain`: strictly positive.
All inputs are finite; a program needn't handle non-finite values.
Results may differ from the reference program's by a relative error of at most 0.0029.
Values may be sent and summed in bfloat16 or wider, within the bound.
A program may use at most 128 MiB of HBM per device.

```python
import math
import jax
import jax.numpy as jnp
from jax import lax

D = 2048
H = 2048
L_DEV = 128
NBURST = 6
ROWS = 4
SEQ = 4096
GROUPS = 32
NDOC = 8


def modulus_law(key, fast_share):
    picker = jax.random.uniform(jax.random.fold_in(key, 11), (H,))
    quick = jax.random.uniform(jax.random.fold_in(key, 12), (H,), minval=0.93, maxval=0.96)
    ceiling = math.log(10.0) / SEQ
    rates = jnp.exp(jax.random.uniform(jax.random.fold_in(key, 13), (H,), minval=math.log(0.1 * ceiling), maxval=math.log(ceiling)))
    return jnp.where(picker < fast_share, quick, jnp.exp(-rates)).astype(jnp.float32)


def draw_modulus(key, part):
    return modulus_law(key, 0.5)


def draw_gain(key, part):
    moduli = modulus_law(key, 0.5)
    key = jax.random.fold_in(key, 3)
    factor = jax.random.uniform(key, (H,), minval=0.5, maxval=1.4)
    return (jnp.sqrt(1.0 - moduli * moduli) * factor).astype(jnp.float32)


def draw_retain(key, part):
    key = jax.random.fold_in(key, 5)
    spots = jax.random.randint(jax.random.fold_in(key, 1), (ROWS, NBURST), 0, SEQ)
    places = jnp.arange(SEQ, dtype=jnp.int32)
    struck = jnp.any(places[None, :, None] == spots[:, None, :], axis=2)
    levels = jax.random.uniform(jax.random.fold_in(key, 2), (ROWS, SEQ), minval=0.5, maxval=0.8)
    return jnp.where(struck, levels, jnp.ones((ROWS, SEQ), jnp.float32)).astype(jnp.float32)


def draw_doc_starts(key, part):
    key = jax.random.fold_in(key, 7)
    others = jax.random.randint(key, (ROWS, NDOC - 1), 1, SEQ).astype(jnp.int32)
    row_index = jnp.arange(ROWS, dtype=jnp.int32)[:, None]
    entry_index = jnp.arange(NDOC - 1, dtype=jnp.int32)[None, :]
    corner = (row_index == 0) & (entry_index == NDOC - 2)
    others = jnp.where(corner, jnp.full((ROWS, NDOC - 1), SEQ - 1, jnp.int32), others)
    return jnp.concatenate([jnp.zeros((ROWS, 1), jnp.int32), others], axis=1)


def draw_row_blocks(key, part):
    key = jax.random.fold_in(key, 9)
    values = jax.random.randint(jax.random.fold_in(key, 1), (ROWS,), 1, max(2, GROUPS // 4) + 1)
    longest = jax.random.randint(jax.random.fold_in(key, 2), (), 0, ROWS)
    return jnp.where(jnp.arange(ROWS) == longest, GROUPS, values).astype(jnp.int32)


def with_spikes(drawn, own_key, source, target, blocks, factor):
    owner, partner = [(jnp.arange(drawn.shape[dim]) // (drawn.shape[dim] // blocks)).reshape([-1 if axis == dim else 1 for axis in range(drawn.ndim)]) for dim in (source, target)]
    chosen = jax.random.permutation(own_key, blocks)[partner]
    strong = (owner == chosen) | (owner == (partner + blocks // 2) % blocks)
    return jnp.where(strong, factor * drawn, drawn)


def shard_levels(key, shape, split, smallest, high):
    level = 1.0
    for axis_at, blocks in split:
        steps = jax.random.uniform(jax.random.fold_in(jax.random.fold_in(key, 6), axis_at), (blocks,), jnp.float32, smallest / len(split), high / len(split))
        level = level * jnp.repeat(jnp.exp(steps), shape[axis_at] // blocks).reshape((-1,) + (1,) * (len(shape) - 1 - axis_at))
    return level


def scatter_about(rng, dims, spread, reach, pieces=(), kind=jnp.bfloat16):
    loudness = shard_levels(rng, dims, pieces, -0.22, 0.18) if pieces else 1.0
    values = jax.random.normal(rng, dims, jnp.float32) * spread * loudness
    return jnp.minimum(jnp.maximum(values, -reach), reach).astype(kind)


def heavy_noise(own_key, extent, width, reach, shards, heavy, kind=jnp.bfloat16):
    array = width * jax.random.normal(own_key, extent, jnp.float32)
    if shards:
        array = array * shard_levels(own_key, extent, shards, -0.22, 0.18)
    return jnp.clip(with_spikes(array, jax.random.fold_in(own_key, 3), *heavy), -reach, reach).astype(kind)


def setup_inputs(seed: int = 0) -> dict:
    splits = jax.random.split(jax.random.key(seed), 10)
    inputs = scatter_about(splits[0], (ROWS, SEQ, 2, H), 1.0, 6.0, ((0, 4), (1, 32), (3, 2)))
    cotangent = heavy_noise(splits[1], (ROWS, SEQ, D), 1.0, 6.0, ((0, 4), (1, 32)), (1, 2, 32, 2.75))
    out_proj = scatter_about(splits[2], (D, 2, H), (2 * H) ** -0.5, 0.09375, ((0, 4), (2, 2)))
    modulus = draw_modulus(jax.random.fold_in(splits[9], 71), 0)
    phase = jnp.clip(jax.random.uniform(splits[4], (H,), jnp.float32, -3.140625, 3.140625), -3.140625, 3.140625)
    gain = draw_gain(jax.random.fold_in(splits[9], 71), 0)
    retain = draw_retain(jax.random.fold_in(splits[9], 71), 0)
    doc_starts = draw_doc_starts(jax.random.fold_in(splits[9], 71), 0)
    row_blocks = draw_row_blocks(jax.random.fold_in(splits[9], 71), 0)
    return dict(inputs=inputs, cotangent=cotangent, out_proj=out_proj, modulus=modulus, phase=phase, gain=gain, retain=retain, doc_starts=doc_starts, row_blocks=row_blocks)


def reference(inputs, cotangent, out_proj, modulus, phase, gain, retain, doc_starts, row_blocks):
    eigen_real = modulus * jnp.cos(phase)
    eigen_imag = modulus * jnp.sin(phase)
    matrix = out_proj.reshape(D, 2 * H)
    position = jnp.arange(SEQ, dtype=jnp.int32)

    def one_row(packed):
        source, upstream, holding, starts, blocks = packed
        alive = position < blocks * L_DEV
        upstream = jnp.where(alive[:, None], upstream, jnp.zeros_like(upstream))
        begins = jnp.any(position[:, None] == starts[None, :].astype(jnp.int32), axis=1)
        keep = holding * (1.0 - begins.astype(jnp.float32))
        source_real = source[:, 0, :].astype(jnp.float32)
        source_imag = source[:, 1, :].astype(jnp.float32)

        def forward(state, item):
            state_real, state_imag = state
            factor, drive_real, drive_imag = item
            new_real = factor * (eigen_real * state_real - eigen_imag * state_imag) + gain * drive_real
            new_imag = factor * (eigen_real * state_imag + eigen_imag * state_real) + gain * drive_imag
            return (new_real, new_imag), (new_real, new_imag)

        empty = jnp.zeros((H,), jnp.float32)
        _, (state_real, state_imag) = lax.scan(forward, (empty, empty), (keep, source_real, source_imag))
        signal = jnp.dot(upstream, matrix, preferred_element_type=jnp.float32)
        next_keep = jnp.concatenate([keep[1:], jnp.zeros((1,), jnp.float32)])

        def backward(adjoint, item):
            adjoint_real, adjoint_imag = adjoint
            factor, signal_real, signal_imag = item
            new_real = signal_real + factor * (eigen_real * adjoint_real + eigen_imag * adjoint_imag)
            new_imag = signal_imag + factor * (eigen_real * adjoint_imag - eigen_imag * adjoint_real)
            return (new_real, new_imag), (new_real, new_imag)

        _, (adjoint_real, adjoint_imag) = lax.scan(
            backward, (empty, empty), (next_keep, signal[:, :H], signal[:, H:]), reverse=True)
        prior_real = jnp.concatenate([jnp.zeros((1, H), jnp.float32), state_real[:-1]], axis=0)
        prior_imag = jnp.concatenate([jnp.zeros((1, H), jnp.float32), state_imag[:-1]], axis=0)
        weight_col = keep[:, None]
        eigen_one = jnp.sum(weight_col * (adjoint_real * prior_real + adjoint_imag * prior_imag), axis=0)
        eigen_two = jnp.sum(weight_col * (adjoint_imag * prior_real - adjoint_real * prior_imag), axis=0)
        gain_part = jnp.sum(adjoint_real * source_real + adjoint_imag * source_imag, axis=0)
        grad_row = jnp.stack([gain * adjoint_real, gain * adjoint_imag], axis=1).astype(jnp.bfloat16)
        half_state = jnp.concatenate([state_real, state_imag], axis=1).astype(jnp.bfloat16)
        proj_row = lax.dot_general(upstream, half_state, (((0,), (0,)), ((), ())),
                                   preferred_element_type=jnp.float32)
        return grad_row, proj_row, eigen_one, eigen_two, gain_part

    grad_rows, proj_rows, eigen_ones, eigen_twos, gain_parts = lax.map(
        one_row, (inputs, cotangent, retain, doc_starts, row_blocks))
    grad_proj = jnp.sum(proj_rows, axis=0).reshape(D, 2, H)
    grad_eigen = jnp.stack([jnp.sum(eigen_ones, axis=0), jnp.sum(eigen_twos, axis=0)])
    return grad_rows, grad_proj, grad_eigen, jnp.sum(gain_parts, axis=0)
```

```python
import functools

import jax
import jax.numpy as jnp
from jax import lax
from jax.experimental import pallas as pl
from jax.experimental.pallas import tpu as pltpu
from jax.sharding import PartitionSpec as P

MESH = pl.DeviceIdType.MESH
F32 = jnp.float32
BF16 = jnp.bfloat16
LANE = 128
SEGS = 8


def grid_of(ctx):
    z = {32: 8, 4: 2, 8: 4}[ctx]
    return ctx // z, z


def cmul(ar, ai, br, bi):
    return ar * br - ai * bi, ar * bi + ai * br


def wide(row, states):
    return jnp.concatenate([row] * (states // LANE), axis=1)


def lanes_of(j):
    return slice(j * LANE, (j + 1) * LANE)


def nearest_last(n):
    return sorted(range(1, n), key=lambda k: -min(k, n - k))


def kernel(
    dims,
    u_ref, cot_ref, w_ref, mod_ref, mask_ref,
    gin_ref, gproj_ref, gsum_ref,
    ur, ui, st_r, st_i, sg_r, sg_i, seg, carry_f, carry_b,
    cga, cslab, ps_send, ps_recv, half, sga, out_x, recv_x, out_y, recv_y, out_z, recv_z,
    msg_fz, msg_fx, msg_bz, msg_bx, msg_sz, msg_sx, msg_sy,
    slab_s, slab_r, ag_s, ag_r, dd_s, dd_r, ps_s, ps_r, sg_s, sg_rs,
    x_s, x_r, y_s, y_r, z_s, z_r,
    fz_s, fz_r, fx_s, fx_r, bz_s, bz_r, bx_s, bx_r, sz_s, sz_r, sx_s, sx_r, sy_s, sy_r,
):
    ny, nx, nz, nc = dims
    tokens, width = cot_ref.shape
    tiles = ur.shape[0]
    states = tiles * LANE
    steps = tokens // SEGS
    slab = width // ny
    part = width // nc
    y = lax.axis_index("dp")
    ctx = lax.axis_index("ctx")
    c = lax.axis_index("chan")
    x, z = ctx // nz, ctx % nz

    def at_z(other):
        return (y, x * nz + other, c)

    def at_x(other):
        return (y, other * nz + z, c)

    def at_y(other):
        return (other, ctx, c)

    sibling = (y, ctx, 1 - c)
    z_peers = [(z + k) % nz for k in nearest_last(nz)]
    x_peers = [(x + k) % nx for k in nearest_last(nx)]
    y_peers = [(y + k) % ny for k in nearest_last(ny)]

    def copy(src, dst, ssem, rsem, device):
        return pltpu.make_async_remote_copy(
            src_ref=src, dst_ref=dst, send_sem=ssem, recv_sem=rsem,
            device_id=device, device_id_type=MESH,
        )

    barrier = pltpu.get_barrier_semaphore()
    greeted = [at_z(p) for p in z_peers] + [at_x(p) for p in x_peers]
    greeted += [at_y(p) for p in y_peers] + [sibling]
    for device in greeted:
        pl.semaphore_signal(barrier, inc=1, device_id=device, device_id_type=MESH)

    alive = mask_ref[1].astype(BF16)
    for h in range(nc):
        cga[z, h] = cot_ref[:, h * part:(h + 1) * part] * wide(alive, part)
    for j in range(tiles):
        ur[j] = u_ref[0, :, lanes_of(j)].astype(F32)
        ui[j] = u_ref[1, :, lanes_of(j)].astype(F32)
    pl.semaphore_wait(barrier, len(greeted))

    def spread(buf, ssem, rsem, mine, peers, where):
        sends = [copy(buf.at[mine], buf.at[mine], ssem.at[p], rsem.at[mine], where(p)) for p in peers]
        for s in sends:
            s.start()
        return sends

    def collect(buf, ssem, rsem, peers, where):
        for p in peers:
            copy(buf.at[p], buf.at[p], ssem.at[p], rsem.at[p], where(p)).wait_recv()

    pending = []

    def slab_view(at):
        per = ny // nc
        lanes = pl.ds(pl.multiple_of((at % per) * slab, LANE), slab)
        return cga.at[z, at // per, :, lanes]

    for p in y_peers:
        s = copy(slab_view(p), cslab.at[y], slab_s.at[p], slab_r.at[y], at_y(p))
        s.start()
        pending.append(s)

    n_right = nz // 2
    n_left = nz - 1 - n_right

    def ring_send(k, to_right):
        slot = (z - k) % nz if to_right else (z + k) % nz
        other = (z + 1) % nz if to_right else (z - 1) % nz
        sem = ag_s.at[0 if to_right else 1, k]
        s = copy(cga.at[slot, c], cga.at[slot, c], sem, ag_r.at[slot], at_z(other))
        s.start()
        pending.append(s)

    def ring_step(k):
        for to_right, count in ((True, n_right), (False, n_left)):
            if 1 <= k <= count:
                slot = (z - k) % nz if to_right else (z + k) % nz
                view = cga.at[slot, c]
                copy(view, view, ag_s.at[0, 0], ag_r.at[slot], sibling).wait_recv()
                if k < count:
                    ring_send(k, to_right)
                s = copy(view, view, dd_s.at[slot], dd_r.at[slot], sibling)
                s.start()
                pending.append(s)
            elif k == 0 and count > 0:
                ring_send(0, to_right)

    ring_step(0)

    lr1 = mod_ref[0:1]
    li1 = mod_ref[1:2]
    gain1 = mod_ref[2:3]
    shape = (SEGS, states)
    lr = jnp.broadcast_to(lr1, shape)
    li = jnp.broadcast_to(li1, shape)
    gain = jnp.broadcast_to(gain1, shape)

    def power(br, bi, n):
        while n > 1:
            br, bi = cmul(br, bi, br, bi)
            n //= 2
        return br, bi

    seg_r, seg_i = power(lr1, li1, steps)
    blk_r, blk_i = power(seg_r, seg_i, SEGS)
    row_r, row_i = power(blk_r, blk_i, nz)

    def rows(ref, i):
        at = pl.ds(i, SEGS, stride=steps)
        return jnp.concatenate([ref[j, at, :] for j in range(tiles)], axis=1)

    def put_rows(ref, i, value):
        for j in range(tiles):
            ref[j, pl.ds(i, SEGS, stride=steps), :] = value[:, lanes_of(j)]

    def keep_at(i):
        return mask_ref[0, pl.ds(i, SEGS, stride=steps), :]

    def summary(i, held):
        sr, si, kp = held
        k = keep_at(i)
        kk = wide(k, states)
        tr, ti = cmul(lr, li, sr, si)
        return kk * tr + gain * rows(ur, i), kk * ti + gain * rows(ui, i), kp * k

    zero = jnp.zeros(shape, F32)
    sr, si, kp = lax.fori_loop(0, steps, summary, (zero, zero, jnp.ones((SEGS, LANE), F32)))
    seg[0] = sr
    seg[1] = si
    seg[2] = wide(kp, states)

    def chain(hr, hi, sign, hold):
        order = range(SEGS) if sign > 0 else range(SEGS - 1, -1, -1)
        for g in order:
            if hold is not None:
                hold[0, g:g + 1] = hr
                hold[1, g:g + 1] = hi
            pr, pi = cmul(seg_r, sign * seg_i, hr, hi)
            kg = seg[2, g:g + 1]
            hr = kg * pr + seg[0, g:g + 1]
            hi = kg * pi + seg[1, g:g + 1]
        return hr, hi

    one = jnp.ones((1, states), F32)
    nil = jnp.zeros((1, states), F32)

    def across(buf, mine, n, ar, ai, sign, keeps):
        order = range(n) if sign > 0 else range(n - 1, -1, -1)
        hr, hi, pr, pi, kr = nil, nil, one, nil, one[:, :LANE]
        er, ei, qr, qi = nil, nil, one, nil
        for k in order:
            here = k == mine
            er = jnp.where(here, hr, er)
            ei = jnp.where(here, hi, ei)
            qr = jnp.where(here, pr, qr)
            qi = jnp.where(here, pi, qi)
            kw = wide(keeps[k], states)
            mr, mi = cmul(ar, sign * ai, hr, hi)
            hr = kw * mr + buf[k, :, 0:states]
            hi = kw * mi + buf[k, :, states:2 * states]
            mr, mi = cmul(ar, sign * ai, pr, pi)
            pr, pi = kw * mr, kw * mi
            kr = kr * keeps[k]
        return hr, hi, er, ei, qr, qi, kr

    br, bi = chain(nil, nil, 1, None)
    kb = one[:, :LANE]
    for g in range(SEGS):
        kb = kb * seg[2, g:g + 1, 0:LANE]
    msg_fz[z, :, 0:states] = br
    msg_fz[z, :, states:2 * states] = bi
    msg_fz[z, :, 2 * states:] = kb
    pending += spread(msg_fz, fz_s, fz_r, z, z_peers, at_z)
    collect(msg_fz, fz_s, fz_r, z_peers, at_z)
    keeps_z = [msg_fz[k, :, 2 * states:] for k in range(nz)]
    hr, hi, er, ei, qr, qi, kx = across(msg_fz, z, nz, blk_r, blk_i, 1, keeps_z)
    msg_fx[x, :, 0:states] = hr
    msg_fx[x, :, states:2 * states] = hi
    msg_fx[x, :, 2 * states:] = kx
    pending += spread(msg_fx, fx_s, fx_r, x, x_peers, at_x)
    collect(msg_fx, fx_s, fx_r, x_peers, at_x)
    keeps_x = [msg_fx[k, :, 2 * states:] for k in range(nx)]
    _, _, fr, fi, _, _, _ = across(msg_fx, x, nx, row_r, row_i, 1, keeps_x)
    mr, mi = cmul(qr, qi, fr, fi)
    chain(mr + er, mi + ei, 1, carry_f)

    def fill(i, held):
        sr, si = held
        kk = wide(keep_at(i), states)
        tr, ti = cmul(lr, li, sr, si)
        sr = kk * tr + gain * rows(ur, i)
        si = kk * ti + gain * rows(ui, i)
        put_rows(st_r, i, sr)
        put_rows(st_i, i, si)
        return sr, si

    lax.fori_loop(0, steps, fill, (carry_f[0], carry_f[1]))
    for k in range(nz):
        half[k, :, 0:LANE] = st_r[k].astype(BF16)
        half[k, :, LANE:] = st_i[k].astype(BF16)
    for p in z_peers:
        s = copy(half.at[p], sga.at[z], sg_s.at[p], sg_rs.at[z], at_z(p))
        s.start()
        pending.append(s)
    sga[z] = half[z]

    ring_step(1)

    for p in y_peers:
        copy(cslab.at[p], cslab.at[p], slab_s.at[p], slab_r.at[p], at_y(p)).wait_recv()
        for h in range(2):
            ps_send[p, h] = jnp.dot(cslab[p], w_ref[h], preferred_element_type=F32).astype(BF16)
            s = copy(ps_send.at[p, h], ps_recv.at[y, h], ps_s.at[p, h], ps_r.at[y, h], at_y(p))
            s.start()
            pending.append(s)
    own = slab_view(y)[...]
    for h, ref in ((0, sg_r), (1, sg_i)):
        share = jnp.dot(own, w_ref[h], preferred_element_type=F32)
        for j in range(tiles):
            ref[j] = share[:, lanes_of(j)]

    for k in range(2, n_right + 1):
        ring_step(k)
    for k in range(1, nz):
        view = cga.at[(z + k) % nz, 1 - c]
        copy(view, view, dd_s.at[0], dd_r.at[(z + k) % nz], sibling).wait_recv()
    collect(sga, sg_s, sg_rs, z_peers, at_z)

    count = nz * tokens
    state_t = sga[...].reshape(count, 2 * LANE).T
    per = ny // nc
    for q in range(ny):
        lanes = slice((q % per) * slab, (q % per + 1) * slab)
        block = cga[:, q // per, :, lanes].reshape(count, slab)
        grad = jnp.dot(state_t, block, preferred_element_type=F32)
        for k in range(nx):
            out_x[k, q] = grad[:, lanes_of(k)]
    for p in x_peers:
        s = copy(out_x.at[p], recv_x.at[x], x_s.at[p], x_r.at[x], at_x(p))
        s.start()
        pending.append(s)

    for p in y_peers:
        for h, ref in ((0, sg_r), (1, sg_i)):
            view = ps_recv.at[p, h]
            copy(view, view, ps_s.at[p, h], ps_r.at[p, h], at_y(p)).wait_recv()
            for j in range(tiles):
                ref[j] += ps_recv[p, h, :, lanes_of(j)].astype(F32)

    def back_summary(n, held):
        i = steps - 1 - n
        hr, hi = held
        kk = wide(keep_at(i), states)
        tr, ti = cmul(lr, -li, rows(sg_r, i) + hr, rows(sg_i, i) + hi)
        return kk * tr, kk * ti

    hr, hi = lax.fori_loop(0, steps, back_summary, (zero, zero))
    seg[0] = hr
    seg[1] = hi
    br, bi = chain(nil, nil, -1, None)
    msg_bz[z, :, 0:states] = br
    msg_bz[z, :, states:] = bi
    pending += spread(msg_bz, bz_s, bz_r, z, z_peers, at_z)
    collect(msg_bz, bz_s, bz_r, z_peers, at_z)
    hr, hi, er, ei, qr, qi, _ = across(msg_bz, z, nz, blk_r, blk_i, -1, keeps_z)
    msg_bx[x, :, 0:states] = hr
    msg_bx[x, :, states:] = hi
    pending += spread(msg_bx, bx_s, bx_r, x, x_peers, at_x)
    collect(msg_bx, bx_s, bx_r, x_peers, at_x)
    _, _, fr, fi, _, _, _ = across(msg_bx, x, nx, row_r, row_i, -1, keeps_x)
    mr, mi = cmul(qr, qi, fr, fi)
    chain(mr + er, mi + ei, -1, carry_b)

    def adjoint_step(i, held, prior_r, prior_i):
        hr, hi, wr, wi, wg = held
        kk = wide(keep_at(i), states)
        ar = rows(sg_r, i) + hr
        ai = rows(sg_i, i) + hi
        put_rows(sg_r, i, gain * ar)
        put_rows(sg_i, i, gain * ai)
        wr = wr + kk * (ar * prior_r + ai * prior_i)
        wi = wi + kk * (ai * prior_r - ar * prior_i)
        wg = wg + ar * rows(ur, i) + ai * rows(ui, i)
        tr, ti = cmul(lr, -li, ar, ai)
        return kk * tr, kk * ti, wr, wi, wg

    def adjoint(n, held):
        i = steps - 1 - n
        return adjoint_step(i, held, rows(st_r, i - 1), rows(st_i, i - 1))

    held = lax.fori_loop(0, steps - 1, adjoint, (carry_b[0], carry_b[1], zero, zero, zero))
    _, _, wr, wi, wg = adjoint_step(0, held, carry_f[0], carry_f[1])
    for j in range(tiles):
        gin_ref[0, :, lanes_of(j)] = sg_r[j].astype(BF16)
        gin_ref[1, :, lanes_of(j)] = sg_i[j].astype(BF16)

    def put(buf, mine, values):
        for k, value in enumerate(values):
            buf[mine, :, k * states:(k + 1) * states] = value

    def total(buf, n):
        out = buf[0]
        for k in range(1, n):
            out = out + buf[k]
        return out

    put(msg_sz, z, [jnp.sum(w, axis=0, keepdims=True) for w in (wr, wi, wg)])
    pending += spread(msg_sz, sz_s, sz_r, z, z_peers, at_z)

    collect(recv_x, x_s, x_r, x_peers, at_x)
    for q in range(ny):
        grad = out_x[x, q]
        for p in x_peers:
            grad = grad + recv_x[p, q]
        out_y[q] = grad
    for p in y_peers:
        s = copy(out_y.at[p], recv_y.at[y], y_s.at[p], y_r.at[y], at_y(p))
        s.start()
        pending.append(s)

    collect(msg_sz, sz_s, sz_r, z_peers, at_z)
    msg_sx[x] = total(msg_sz, nz)
    pending += spread(msg_sx, sx_s, sx_r, x, x_peers, at_x)
    collect(msg_sx, sx_s, sx_r, x_peers, at_x)
    msg_sy[y] = total(msg_sx, nx)
    pending += spread(msg_sy, sy_s, sy_r, y, y_peers, at_y)

    collect(recv_y, y_s, y_r, y_peers, at_y)
    grad = out_y[y]
    for p in y_peers:
        grad = grad + recv_y[p]
    out_z[...] = grad.T.reshape(out_z.shape)
    for p in z_peers:
        s = copy(out_z.at[p], recv_z.at[z], z_s.at[p], z_r.at[z], at_z(p))
        s.start()
        pending.append(s)
    recv_z[z] = out_z[z]

    collect(msg_sy, sy_s, sy_r, y_peers, at_y)
    gsum_ref[...] = total(msg_sy, ny)

    collect(recv_z, z_s, z_r, z_peers, at_z)
    for k in range(nz):
        for h in range(2):
            gproj_ref[h, :, lanes_of(k)] = recv_z[k, :, lanes_of(h)]

    for s in pending:
        s.wait_send()


def body(dims, inputs, cotangent, out_proj, modulus, phase, gain, retain, doc_starts, row_blocks):
    ny, nx, nz, nc = dims
    _, tokens, _, states = inputs.shape
    width = cotangent.shape[2]
    slab = width // ny
    index = lax.axis_index("ctx")
    position = index * tokens + jnp.arange(tokens, dtype=jnp.int32)
    begins = jnp.any(position[:, None] == doc_starts, axis=1)
    keep = retain[0] * (1.0 - begins.astype(F32))
    alive = (index < row_blocks[0]).astype(F32)
    mask = jnp.stack(
        [jnp.broadcast_to(keep[:, None], (tokens, LANE)), jnp.full((tokens, LANE), alive)]
    )
    coefficients = jnp.stack([modulus * jnp.cos(phase), modulus * jnp.sin(phase), gain])
    drive = inputs[0].transpose(1, 0, 2)
    weight = out_proj.transpose(1, 0, 2)
    rows_z = LANE // nz
    dma = pltpu.SemaphoreType.DMA

    def pair(*shape):
        return [dma(shape), dma(shape)]

    line = 2 * states + LANE
    scratch = [
        *[pltpu.VMEM((states // LANE, tokens, LANE), F32) for _ in range(6)],
        pltpu.VMEM((3, SEGS, states), F32),
        pltpu.VMEM((2, SEGS, states), F32), pltpu.VMEM((2, SEGS, states), F32),
        pltpu.VMEM((nz, nc, tokens, width // nc), BF16),
        pltpu.VMEM((ny, tokens, slab), BF16),
        pltpu.VMEM((ny, 2, tokens, states), BF16), pltpu.VMEM((ny, 2, tokens, states), BF16),
        pltpu.VMEM((nz, tokens, 2 * LANE), BF16), pltpu.VMEM((nz, tokens, 2 * LANE), BF16),
        pltpu.VMEM((nx, ny, 2 * LANE, LANE), F32), pltpu.VMEM((nx, ny, 2 * LANE, LANE), F32),
        pltpu.VMEM((ny, 2 * LANE, LANE), F32), pltpu.VMEM((ny, 2 * LANE, LANE), F32),
        pltpu.VMEM((nz, rows_z, 2 * LANE), F32), pltpu.VMEM((nz, rows_z, 2 * LANE), F32),
        pltpu.VMEM((nz, 1, line), F32), pltpu.VMEM((nx, 1, line), F32),
        pltpu.VMEM((nz, 1, 2 * states), F32), pltpu.VMEM((nx, 1, 2 * states), F32),
        pltpu.VMEM((nz, 1, 3 * states), F32), pltpu.VMEM((nx, 1, 3 * states), F32),
        pltpu.VMEM((ny, 1, 3 * states), F32),
        *pair(ny), dma((2, nz)), dma((nz,)), *pair(nz), *pair(ny, 2), *pair(nz),
        *pair(nx), *pair(ny), *pair(nz),
        *pair(nz), *pair(nx), *pair(nz), *pair(nx), *pair(nz), *pair(nx), *pair(ny),
    ]
    whole = pl.BlockSpec(memory_space=pltpu.VMEM)
    grad_inputs, grad_proj, sums = pl.pallas_call(
        functools.partial(kernel, dims),
        out_shape=(
            jax.ShapeDtypeStruct((2, tokens, states), BF16),
            jax.ShapeDtypeStruct((2, rows_z, states), F32),
            jax.ShapeDtypeStruct((1, 3 * states), F32),
        ),
        in_specs=[whole] * 5,
        out_specs=(whole,) * 3,
        scratch_shapes=scratch,
        compiler_params=pltpu.CompilerParams(
            collective_id=0, has_side_effects=True, vmem_limit_bytes=56 * 1024 * 1024
        ),
    )(drive, cotangent[0], weight, coefficients, mask)
    sums = sums.reshape(3, states)
    return (
        grad_inputs.transpose(1, 0, 2)[None],
        grad_proj.transpose(1, 0, 2),
        sums[:2],
        sums[2],
    )


def solution(mesh):
    sizes = mesh.shape
    nx, nz = grid_of(sizes["ctx"])
    dims = (sizes["dp"], nx, nz, sizes["chan"])
    return jax.shard_map(
        functools.partial(body, dims),
        mesh=mesh,
        in_specs=(
            P("dp", "ctx", None, "chan"),
            P("dp", "ctx", None),
            P("dp", None, "chan"),
            P("chan"),
            P("chan"),
            P("chan"),
            P("dp", "ctx"),
            P("dp", None),
            P("dp"),
        ),
        out_specs=(
            P("dp", "ctx", None, "chan"),
            P(("dp", "ctx"), None, "chan"),
            P(None, "chan"),
            P("chan"),
        ),
        check_vma=False,
    )
```

```python
import functools

import jax
import jax.numpy as jnp
from jax import lax
from jax.experimental import pallas as pl
from jax.experimental.pallas import tpu as pltpu
from jax.sharding import PartitionSpec as P

MESH = pl.DeviceIdType.MESH
F32 = jnp.float32
BF16 = jnp.bfloat16
LANE = 128
SEGS = 8


def grid_of(ctx):
    z = {32: 8, 4: 2, 8: 4}[ctx]
    return ctx // z, z


def cmul(ar, ai, br, bi):
    return ar * br - ai * bi, ar * bi + ai * br


def wide(row, states):
    return jnp.concatenate([row] * (states // LANE), axis=1)


def lanes_of(j):
    return slice(j * LANE, (j + 1) * LANE)


def nearest_last(n):
    return sorted(range(1, n), key=lambda k: -min(k, n - k))


def kernel(
    dims,
    starts_ref, blocks_ref, mod_ref, phase_ref, gain_ref, retain_ref, u_hbm, cot_hbm, w_hbm,
    gin_ref, gproj_ref, geig_ref, ggain_ref,
    u_raw, cot_raw, w_raw, w_wide, w_ref, mask,
    ur, ui, st_r, st_i, sg_r, sg_i, seg, carry_f, carry_b,
    cga, cslab, ps_send, ps_recv, half, sga, grads, out_x, recv_x, out_y, recv_y, out_z, recv_z,
    msg_fz, msg_fx, msg_bz, msg_bx, msg_sz, msg_sx, msg_sy,
    load_s, slab_s, slab_r, ag_s, ag_r, dd_s, dd_r, ps_s, ps_r, sg_s, sg_rs,
    x_s, x_r, y_s, y_r, z_s, z_r,
    fz_s, fz_r, fx_s, fx_r, bz_s, bz_r, bx_s, bx_r, sz_s, sz_r, sx_s, sx_r, sy_s, sy_r,
):
    ny, nx, nz, nc = dims
    tokens, width = cot_raw.shape
    tiles = ur.shape[0]
    states = tiles * LANE
    steps = tokens // SEGS
    slab = width // ny
    stages = ny // nc
    y = lax.axis_index("dp")
    ctx = lax.axis_index("ctx")
    c = lax.axis_index("chan")
    x, z = ctx // nz, ctx % nz

    def at_z(other):
        return (y, x * nz + other, c)

    def at_x(other):
        return (y, other * nz + z, c)

    def at_y(other):
        return (other, ctx, c)

    sibling = (y, ctx, 1 - c)
    z_peers = [(z + k) % nz for k in nearest_last(nz)]
    x_peers = [(x + k) % nx for k in nearest_last(nx)]
    y_peers = [(y + k) % ny for k in nearest_last(ny)]

    def copy(src, dst, ssem, rsem, device):
        return pltpu.make_async_remote_copy(
            src_ref=src, dst_ref=dst, send_sem=ssem, recv_sem=rsem,
            device_id=device, device_id_type=MESH,
        )

    barrier = pltpu.get_barrier_semaphore()
    greeted = [at_z(p) for p in z_peers] + [at_x(p) for p in x_peers]
    greeted += [at_y(p) for p in y_peers] + [sibling]
    for device in greeted:
        pl.semaphore_signal(barrier, inc=1, device_id=device, device_id_type=MESH)
    load_cot = pltpu.make_async_copy(cot_hbm, cot_raw, load_s.at[0])
    load_u = pltpu.make_async_copy(u_hbm, u_raw, load_s.at[1])
    load_w = pltpu.make_async_copy(w_hbm, w_raw, load_s.at[2])
    load_cot.start()
    load_u.start()
    load_w.start()

    row = lax.broadcasted_iota(jnp.int32, (1, tokens), 1) + ctx * tokens
    keep = retain_ref[...]
    for k in range(starts_ref.shape[1]):
        keep = jnp.where(row == starts_ref[0, k], 0.0, keep)
    mask[...] = jnp.broadcast_to(keep, (LANE, tokens)).T

    alive = jnp.where(ctx < blocks_ref[0], 1.0, 0.0).astype(F32)
    alive = jnp.full((tokens, slab), alive, F32).astype(BF16)
    load_cot.wait()
    for q in range(ny):
        cga[z, q] = cot_raw[:, q * slab:(q + 1) * slab] * alive
    pl.semaphore_wait(barrier, len(greeted))

    def spread(buf, ssem, rsem, mine, peers, where):
        sends = [copy(buf.at[mine], buf.at[mine], ssem.at[p], rsem.at[mine], where(p)) for p in peers]
        for s in sends:
            s.start()
        return sends

    def collect(buf, ssem, rsem, peers, where):
        for p in peers:
            copy(buf.at[p], buf.at[p], ssem.at[p], rsem.at[p], where(p)).wait_recv()

    pending = []

    for p in y_peers:
        s = copy(cga.at[z, p], cslab.at[y], slab_s.at[p], slab_r.at[y], at_y(p))
        s.start()
        pending.append(s)

    n_right = nz // 2
    n_left = nz - 1 - n_right

    def ring_step(stage, k):
        q = stage * nc + c
        for way, count in ((0, n_right), (1, n_left)):
            sign = -1 if way == 0 else 1
            slot = (z + sign * k) % nz
            view = cga.at[slot, q]
            if 1 <= k <= count:
                copy(view, view, ag_s.at[stage, way, 0], ag_r.at[stage, slot], sibling).wait_recv()
            if k < count:
                s = copy(view, view, ag_s.at[stage, way, k], ag_r.at[stage, slot], at_z((z - sign) % nz))
                s.start()
                pending.append(s)
            if 1 <= k <= count:
                s = copy(view, view, dd_s.at[stage, slot], dd_r.at[stage, slot], sibling)
                s.start()
                pending.append(s)

    def ring_end(stage):
        q = stage * nc + 1 - c
        for k in range(1, nz):
            slot = (z + k) % nz
            view = cga.at[slot, q]
            copy(view, view, dd_s.at[stage, slot], dd_r.at[stage, slot], sibling).wait_recv()

    todo = [(stage, k) for stage in range(stages) for k in range(n_right + 1)]

    def advance(count=1, stage=None):
        while todo and (count > 0 or (stage is not None and todo[0][0] <= stage)):
            ring_step(*todo.pop(0))
            count -= 1

    advance()

    lr1 = mod_ref[...] * jnp.cos(phase_ref[...])
    li1 = mod_ref[...] * jnp.sin(phase_ref[...])
    shape = (SEGS, states)
    lr = jnp.broadcast_to(lr1, shape)
    li = jnp.broadcast_to(li1, shape)
    gain = jnp.broadcast_to(gain_ref[...], shape)

    def power(br, bi, n):
        while n > 1:
            br, bi = cmul(br, bi, br, bi)
            n //= 2
        return br, bi

    seg_r, seg_i = power(lr1, li1, steps)
    blk_r, blk_i = power(seg_r, seg_i, SEGS)
    row_r, row_i = power(blk_r, blk_i, nz)

    load_u.wait()
    drive = u_raw[...].astype(F32)
    for j in range(tiles):
        ur[j] = drive[:, 0, lanes_of(j)]
        ui[j] = drive[:, 1, lanes_of(j)]

    def rows(ref, i):
        at = pl.ds(i, SEGS, stride=steps)
        return jnp.concatenate([ref[j, at, :] for j in range(tiles)], axis=1)

    def put_rows(ref, i, value):
        for j in range(tiles):
            ref[j, pl.ds(i, SEGS, stride=steps), :] = value[:, lanes_of(j)]

    def keep_at(i):
        return mask[pl.ds(i, SEGS, stride=steps), :]

    def summary(i, held):
        sr, si, kp = held
        k = keep_at(i)
        kk = wide(k, states)
        tr, ti = cmul(lr, li, sr, si)
        return kk * tr + gain * rows(ur, i), kk * ti + gain * rows(ui, i), kp * k

    zero = jnp.zeros(shape, F32)
    sr, si, kp = lax.fori_loop(0, steps, summary, (zero, zero, jnp.ones((SEGS, LANE), F32)))
    seg[0] = sr
    seg[1] = si
    seg[2] = wide(kp, states)

    def chain(hr, hi, sign, hold):
        order = range(SEGS) if sign > 0 else range(SEGS - 1, -1, -1)
        for g in order:
            if hold is not None:
                hold[0, g:g + 1] = hr
                hold[1, g:g + 1] = hi
            pr, pi = cmul(seg_r, sign * seg_i, hr, hi)
            kg = seg[2, g:g + 1]
            hr = kg * pr + seg[0, g:g + 1]
            hi = kg * pi + seg[1, g:g + 1]
        return hr, hi

    one = jnp.ones((1, states), F32)
    nil = jnp.zeros((1, states), F32)

    def across(buf, mine, n, ar, ai, sign, keeps):
        order = range(n) if sign > 0 else range(n - 1, -1, -1)
        hr, hi, pr, pi, kr = nil, nil, one, nil, one[:, :LANE]
        er, ei, qr, qi = nil, nil, one, nil
        for k in order:
            here = k == mine
            er = jnp.where(here, hr, er)
            ei = jnp.where(here, hi, ei)
            qr = jnp.where(here, pr, qr)
            qi = jnp.where(here, pi, qi)
            kw = wide(keeps[k], states)
            mr, mi = cmul(ar, sign * ai, hr, hi)
            hr = kw * mr + buf[k, :, 0:states]
            hi = kw * mi + buf[k, :, states:2 * states]
            mr, mi = cmul(ar, sign * ai, pr, pi)
            pr, pi = kw * mr, kw * mi
            kr = kr * keeps[k]
        return hr, hi, er, ei, qr, qi, kr

    br, bi = chain(nil, nil, 1, None)
    kb = one[:, :LANE]
    for g in range(SEGS):
        kb = kb * seg[2, g:g + 1, 0:LANE]
    msg_fz[z, :, 0:states] = br
    msg_fz[z, :, states:2 * states] = bi
    msg_fz[z, :, 2 * states:] = kb
    pending += spread(msg_fz, fz_s, fz_r, z, z_peers, at_z)

    load_w.wait()
    depth = w_wide.shape[1]

    def part_weights(n, carry):
        at = pl.ds(pl.multiple_of(n * depth, depth), depth)
        block = w_raw[at].astype(F32)
        w_wide[0] = block[:, 0, :]
        w_wide[1] = block[:, 1, :]
        w_ref[0, at, :] = w_wide[0].astype(BF16)
        w_ref[1, at, :] = w_wide[1].astype(BF16)
        return carry

    lax.fori_loop(0, slab // depth, part_weights, 0)
    advance()

    collect(msg_fz, fz_s, fz_r, z_peers, at_z)
    keeps_z = [msg_fz[k, :, 2 * states:] for k in range(nz)]
    hr, hi, er, ei, qr, qi, kx = across(msg_fz, z, nz, blk_r, blk_i, 1, keeps_z)
    msg_fx[x, :, 0:states] = hr
    msg_fx[x, :, states:2 * states] = hi
    msg_fx[x, :, 2 * states:] = kx
    pending += spread(msg_fx, fx_s, fx_r, x, x_peers, at_x)

    for p in y_peers:
        copy(cslab.at[p], cslab.at[p], slab_s.at[p], slab_r.at[p], at_y(p)).wait_recv()
        for h in range(2):
            ps_send[p, h] = jnp.dot(cslab[p], w_ref[h], preferred_element_type=F32).astype(BF16)
            s = copy(ps_send.at[p, h], ps_recv.at[y, h], ps_s.at[p, h], ps_r.at[y, h], at_y(p))
            s.start()
            pending.append(s)
    advance()

    collect(msg_fx, fx_s, fx_r, x_peers, at_x)
    keeps_x = [msg_fx[k, :, 2 * states:] for k in range(nx)]
    _, _, fr, fi, _, _, _ = across(msg_fx, x, nx, row_r, row_i, 1, keeps_x)
    mr, mi = cmul(qr, qi, fr, fi)
    chain(mr + er, mi + ei, 1, carry_f)

    def fill(i, held):
        sr, si = held
        kk = wide(keep_at(i), states)
        tr, ti = cmul(lr, li, sr, si)
        sr = kk * tr + gain * rows(ur, i)
        si = kk * ti + gain * rows(ui, i)
        put_rows(st_r, i, sr)
        put_rows(st_i, i, si)
        return sr, si

    lax.fori_loop(0, steps, fill, (carry_f[0], carry_f[1]))
    for k in range(nz):
        half[k, :, 0:LANE] = st_r[k].astype(BF16)
        half[k, :, LANE:] = st_i[k].astype(BF16)
    for p in z_peers:
        s = copy(half.at[p], sga.at[z], sg_s.at[p], sg_rs.at[z], at_z(p))
        s.start()
        pending.append(s)
    sga[z] = half[z]

    own = cga[z, y]
    for h, ref in ((0, sg_r), (1, sg_i)):
        share = jnp.dot(own, w_ref[h], preferred_element_type=F32)
        for j in range(tiles):
            ref[j] = share[:, lanes_of(j)]
    advance(0, 0)
    advance()

    def project(stage):
        count = nz * tokens
        state_t = sga[...].reshape(count, 2 * LANE).T
        slabs = range(stage * nc, (stage + 1) * nc)
        for q in slabs:
            block = cga[:, q].reshape(count, slab)
            grad = jnp.dot(state_t, block, preferred_element_type=F32)
            for k in range(nx):
                grads[q, k] = grad[:, lanes_of(k)]
                out_x[k, q] = grad[:, lanes_of(k)].astype(BF16)
        at = pl.ds(stage * nc, nc)
        for p in x_peers:
            s = copy(out_x.at[p, at], recv_x.at[x, at], x_s.at[stage, p], x_r.at[stage, x], at_x(p))
            s.start()
            pending.append(s)

    ring_end(0)
    collect(sga, sg_s, sg_rs, z_peers, at_z)
    project(0)
    advance()

    for p in y_peers:
        for h, ref in ((0, sg_r), (1, sg_i)):
            view = ps_recv.at[p, h]
            copy(view, view, ps_s.at[p, h], ps_r.at[p, h], at_y(p)).wait_recv()
            for j in range(tiles):
                ref[j] += ps_recv[p, h, :, lanes_of(j)].astype(F32)

    def back_summary(n, held):
        i = steps - 1 - n
        hr, hi = held
        kk = wide(keep_at(i), states)
        tr, ti = cmul(lr, -li, rows(sg_r, i) + hr, rows(sg_i, i) + hi)
        return kk * tr, kk * ti

    hr, hi = lax.fori_loop(0, steps, back_summary, (zero, zero))
    seg[0] = hr
    seg[1] = hi
    br, bi = chain(nil, nil, -1, None)
    msg_bz[z, :, 0:states] = br
    msg_bz[z, :, states:] = bi
    pending += spread(msg_bz, bz_s, bz_r, z, z_peers, at_z)
    advance()
    collect(msg_bz, bz_s, bz_r, z_peers, at_z)
    hr, hi, er, ei, qr, qi, _ = across(msg_bz, z, nz, blk_r, blk_i, -1, keeps_z)
    msg_bx[x, :, 0:states] = hr
    msg_bx[x, :, states:] = hi
    pending += spread(msg_bx, bx_s, bx_r, x, x_peers, at_x)
    advance()
    collect(msg_bx, bx_s, bx_r, x_peers, at_x)
    _, _, fr, fi, _, _, _ = across(msg_bx, x, nx, row_r, row_i, -1, keeps_x)
    mr, mi = cmul(qr, qi, fr, fi)
    chain(mr + er, mi + ei, -1, carry_b)

    def adjoint_step(i, held, prior_r, prior_i):
        hr, hi, wr, wi, wg = held
        kk = wide(keep_at(i), states)
        ar = rows(sg_r, i) + hr
        ai = rows(sg_i, i) + hi
        put_rows(sg_r, i, gain * ar)
        put_rows(sg_i, i, gain * ai)
        wr = wr + kk * (ar * prior_r + ai * prior_i)
        wi = wi + kk * (ai * prior_r - ar * prior_i)
        wg = wg + ar * rows(ur, i) + ai * rows(ui, i)
        tr, ti = cmul(lr, -li, ar, ai)
        return kk * tr, kk * ti, wr, wi, wg

    def adjoint(n, held):
        i = steps - 1 - n
        return adjoint_step(i, held, rows(st_r, i - 1), rows(st_i, i - 1))

    held = lax.fori_loop(0, steps - 1, adjoint, (carry_b[0], carry_b[1], zero, zero, zero))
    _, _, wr, wi, wg = adjoint_step(0, held, carry_f[0], carry_f[1])

    def put(buf, mine, values):
        for k, value in enumerate(values):
            buf[mine, :, k * states:(k + 1) * states] = value

    def total(buf, n):
        out = buf[0]
        for k in range(1, n):
            out = out + buf[k]
        return out

    put(msg_sz, z, [jnp.sum(w, axis=0, keepdims=True) for w in (wr, wi, wg)])
    pending += spread(msg_sz, sz_s, sz_r, z, z_peers, at_z)

    for stage in range(1, stages):
        advance(0, stage)
        ring_end(stage)
        project(stage)

    collect(msg_sz, sz_s, sz_r, z_peers, at_z)
    msg_sx[x] = total(msg_sz, nz)
    pending += spread(msg_sx, sx_s, sx_r, x, x_peers, at_x)

    for j in range(tiles):
        gin_ref[:, 0, lanes_of(j)] = sg_r[j].astype(BF16)
        gin_ref[:, 1, lanes_of(j)] = sg_i[j].astype(BF16)

    for stage in range(stages):
        at = pl.ds(stage * nc, nc)
        for p in x_peers:
            view = recv_x.at[p, at]
            copy(view, view, x_s.at[stage, p], x_r.at[stage, p], at_x(p)).wait_recv()
    for q in range(ny):
        grad = grads[q, x]
        for p in x_peers:
            grad = grad + recv_x[p, q].astype(F32)
        out_y[q] = grad
    for p in y_peers:
        s = copy(out_y.at[p], recv_y.at[y], y_s.at[p], y_r.at[y], at_y(p))
        s.start()
        pending.append(s)

    collect(msg_sx, sx_s, sx_r, x_peers, at_x)
    msg_sy[y] = total(msg_sx, nx)
    pending += spread(msg_sy, sy_s, sy_r, y, y_peers, at_y)

    collect(recv_y, y_s, y_r, y_peers, at_y)
    grad = out_y[y]
    for p in y_peers:
        grad = grad + recv_y[p]
    out_z[...] = grad.T.reshape(out_z.shape)
    for p in z_peers:
        s = copy(out_z.at[p], recv_z.at[z], z_s.at[p], z_r.at[z], at_z(p))
        s.start()
        pending.append(s)
    recv_z[z] = out_z[z]

    collect(msg_sy, sy_s, sy_r, y_peers, at_y)
    sums = total(msg_sy, ny)
    geig_ref[0:1] = sums[:, 0:states]
    geig_ref[1:2] = sums[:, states:2 * states]
    ggain_ref[...] = sums[:, 2 * states:]

    collect(recv_z, z_s, z_r, z_peers, at_z)
    for k in range(nz):
        for h in range(2):
            gproj_ref[:, h, lanes_of(k)] = recv_z[k, :, lanes_of(h)]

    for s in pending:
        s.wait_send()


def body(dims, inputs, cotangent, out_proj, modulus, phase, gain, retain, doc_starts, row_blocks):
    ny, nx, nz, nc = dims
    _, tokens, _, states = inputs.shape
    width = cotangent.shape[2]
    slab = width // ny
    stages = ny // nc
    rows_z = LANE // nz
    dma = pltpu.SemaphoreType.DMA

    def pair(*shape):
        return [dma(shape), dma(shape)]

    line = 2 * states + LANE
    scratch = [
        pltpu.VMEM((tokens, 2, states), BF16),
        pltpu.VMEM((tokens, width), BF16),
        pltpu.VMEM((slab, 2, states), BF16),
        pltpu.VMEM((2, LANE, states), F32),
        pltpu.VMEM((2, slab, states), BF16),
        pltpu.VMEM((tokens, LANE), F32),
        *[pltpu.VMEM((states // LANE, tokens, LANE), F32) for _ in range(6)],
        pltpu.VMEM((3, SEGS, states), F32),
        pltpu.VMEM((2, SEGS, states), F32), pltpu.VMEM((2, SEGS, states), F32),
        pltpu.VMEM((nz, ny, tokens, slab), BF16),
        pltpu.VMEM((ny, tokens, slab), BF16),
        pltpu.VMEM((ny, 2, tokens, states), BF16), pltpu.VMEM((ny, 2, tokens, states), BF16),
        pltpu.VMEM((nz, tokens, 2 * LANE), BF16), pltpu.VMEM((nz, tokens, 2 * LANE), BF16),
        pltpu.VMEM((ny, nx, 2 * LANE, LANE), F32),
        pltpu.VMEM((nx, ny, 2 * LANE, LANE), BF16), pltpu.VMEM((nx, ny, 2 * LANE, LANE), BF16),
        pltpu.VMEM((ny, 2 * LANE, LANE), F32), pltpu.VMEM((ny, 2 * LANE, LANE), F32),
        pltpu.VMEM((nz, rows_z, 2 * LANE), F32), pltpu.VMEM((nz, rows_z, 2 * LANE), F32),
        pltpu.VMEM((nz, 1, line), F32), pltpu.VMEM((nx, 1, line), F32),
        pltpu.VMEM((nz, 1, 2 * states), F32), pltpu.VMEM((nx, 1, 2 * states), F32),
        pltpu.VMEM((nz, 1, 3 * states), F32), pltpu.VMEM((nx, 1, 3 * states), F32),
        pltpu.VMEM((ny, 1, 3 * states), F32),
        dma((3,)), *pair(ny), dma((stages, 2, nz)), dma((stages, nz)), *pair(stages, nz),
        *pair(ny, 2), *pair(nz), *pair(stages, nx), *pair(ny), *pair(nz),
        *pair(nz), *pair(nx), *pair(nz), *pair(nx), *pair(nz), *pair(nx), *pair(ny),
    ]
    vmem = pl.BlockSpec(memory_space=pltpu.VMEM)
    smem = pl.BlockSpec(memory_space=pltpu.SMEM)
    hbm = pl.BlockSpec(memory_space=pl.ANY)
    grad_inputs, grad_proj, grad_eigen, grad_gain = pl.pallas_call(
        functools.partial(kernel, dims),
        out_shape=(
            jax.ShapeDtypeStruct((tokens, 2, states), BF16),
            jax.ShapeDtypeStruct((rows_z, 2, states), F32),
            jax.ShapeDtypeStruct((2, states), F32),
            jax.ShapeDtypeStruct((1, states), F32),
        ),
        in_specs=[smem, smem, vmem, vmem, vmem, vmem, hbm, hbm, hbm],
        out_specs=(vmem,) * 4,
        scratch_shapes=scratch,
        compiler_params=pltpu.CompilerParams(
            collective_id=0, has_side_effects=True, vmem_limit_bytes=56 * 1024 * 1024
        ),
    )(
        doc_starts, row_blocks, modulus[None], phase[None], gain[None], retain,
        inputs[0], cotangent[0], out_proj,
    )
    return grad_inputs[None], grad_proj, grad_eigen, grad_gain[0]


def solution(mesh):
    sizes = mesh.shape
    nx, nz = grid_of(sizes["ctx"])
    dims = (sizes["dp"], nx, nz, sizes["chan"])
    return jax.shard_map(
        functools.partial(body, dims),
        mesh=mesh,
        in_specs=(
            P("dp", "ctx", None, "chan"),
            P("dp", "ctx", None),
            P("dp", None, "chan"),
            P("chan"),
            P("chan"),
            P("chan"),
            P("dp", "ctx"),
            P("dp", None),
            P("dp"),
        ),
        out_specs=(
            P("dp", "ctx", None, "chan"),
            P(("dp", "ctx"), None, "chan"),
            P(None, "chan"),
            P("chan"),
        ),
        check_vma=False,
    )
```

```python
import functools

import jax
import jax.numpy as jnp
from jax import lax
from jax.experimental import pallas as pl
from jax.experimental.pallas import tpu as pltpu
from jax.sharding import PartitionSpec as P

MESH = pl.DeviceIdType.MESH
F32 = jnp.float32
BF16 = jnp.bfloat16
LANE = 128
SEGS = 8


def grid_of(ctx):
    z = {32: 8, 4: 2, 8: 4}[ctx]
    return ctx // z, z


def cmul(ar, ai, br, bi):
    return ar * br - ai * bi, ar * bi + ai * br


def wide(row, states):
    return jnp.concatenate([row] * (states // LANE), axis=1)


def lanes_of(j):
    return slice(j * LANE, (j + 1) * LANE)


def nearest_last(n):
    return sorted(range(1, n), key=lambda k: -min(k, n - k))


def kernel(
    dims,
    starts_ref, blocks_ref, mod_ref, phase_ref, gain_ref, retain_ref, u_hbm, cot_hbm, w_hbm,
    gin_ref, gproj_ref, geig_ref, ggain_ref,
    u_raw, cot_raw, w_raw, w_wide, w_ref, mask,
    ur, ui, st_r, st_i, sg_r, sg_i, seg, bseg, carry_f, carry_b,
    cga, cslab, ps_send, ps_recv, half, sga, grads, out_p, recv_p, out_z, recv_z,
    msg_fz, msg_fx, msg_bz, msg_bx, msg_sy,
    load_s, slab_s, slab_r, ag_s, ag_r, dd_s, dd_r, ps_s, ps_r, sg_s, sg_rs,
    p_s, p_r, z_s, z_r,
    fz_s, fz_r, fx_s, fx_r, bz_s, bz_r, bx_s, bx_r, sy_s, sy_r,
):
    ny, nx, nz, nc = dims
    tokens, width = cot_raw.shape
    tiles = ur.shape[0]
    states = tiles * LANE
    steps = tokens // SEGS
    slab = width // ny
    stages = ny // nc
    y = lax.axis_index("dp")
    ctx = lax.axis_index("ctx")
    c = lax.axis_index("chan")
    x, z = ctx // nz, ctx % nz

    def at_z(other):
        return (y, x * nz + other, c)

    def at_x(other):
        return (y, other * nz + z, c)

    def at_y(other):
        return (other, ctx, c)

    def at_yx(row, col):
        return (row, col * nz + z, c)

    sibling = (y, ctx, 1 - c)
    z_peers = [(z + k) % nz for k in nearest_last(nz)]
    x_peers = [(x + k) % nx for k in nearest_last(nx)]
    y_peers = [(y + k) % ny for k in nearest_last(ny)]

    yx_peers = [(p, q) for p in y_peers for q in x_peers]

    def copy(src, dst, ssem, rsem, device):
        return pltpu.make_async_remote_copy(
            src_ref=src, dst_ref=dst, send_sem=ssem, recv_sem=rsem,
            device_id=device, device_id_type=MESH,
        )

    barrier = pltpu.get_barrier_semaphore()
    greeted = [at_z(p) for p in z_peers] + [at_x(p) for p in x_peers]
    greeted += [at_y(p) for p in y_peers] + [sibling] + [at_yx(*p) for p in yx_peers]
    for device in greeted:
        pl.semaphore_signal(barrier, inc=1, device_id=device, device_id_type=MESH)
    load_cot = pltpu.make_async_copy(cot_hbm, cot_raw, load_s.at[0])
    load_u = pltpu.make_async_copy(u_hbm, u_raw, load_s.at[1])
    load_w = pltpu.make_async_copy(w_hbm, w_raw, load_s.at[2])
    load_cot.start()
    load_u.start()
    load_w.start()

    alive = jnp.where(ctx < blocks_ref[...], 1.0, 0.0)
    alive = jnp.broadcast_to(alive, (tokens, slab)).astype(BF16)
    load_cot.wait()
    for q in range(ny):
        cga[z, q] = cot_raw[:, q * slab:(q + 1) * slab] * alive
    pl.semaphore_wait(barrier, len(greeted))

    def arrived(view, rsem):
        copy(view, view, rsem, rsem, sibling).wait_recv()

    def departed(view, ssem):
        pending.append(copy(view, view, ssem, ssem, sibling))

    def settle():
        for s in pending:
            s.wait_send()
        pending.clear()

    def spread(buf, ssem, rsem, mine, peers, where):
        for p in peers:
            copy(buf.at[mine], buf.at[mine], ssem, rsem, where(p)).start()
        if peers:
            departed(buf.at[pl.ds(0, len(peers))], ssem)

    def collect(buf, rsem, peers):
        if peers:
            arrived(buf.at[pl.ds(0, len(peers))], rsem)

    pending = []

    for p in y_peers:
        copy(cga.at[z, p], cslab.at[y], slab_s, slab_r.at[y], at_y(p)).start()
    departed(cslab.at[pl.ds(0, ny - 1)], slab_s)

    n_right = nz // 2
    n_left = nz - 1 - n_right

    def ring_step(stage, k):
        q = stage * nc + c
        for way, count in ((0, n_right), (1, n_left)):
            sign = -1 if way == 0 else 1
            slot = (z + sign * k) % nz
            view = cga.at[slot, q]
            if 1 <= k <= count:
                arrived(view, ag_r.at[stage, slot])
            if k < count:
                copy(view, view, ag_s.at[stage], ag_r.at[stage, slot], at_z((z - sign) % nz)).start()
            if 1 <= k <= count:
                copy(view, view, dd_s.at[stage], dd_r.at[stage], sibling).start()
        if k == n_right:
            departed(cga.at[pl.ds(0, nz - 1), q], ag_s.at[stage])
            departed(cga.at[pl.ds(0, nz - 1), q], dd_s.at[stage])

    def ring_end(stage):
        arrived(cga.at[pl.ds(0, nz - 1), stage * nc + 1 - c], dd_r.at[stage])

    todo = sorted(
        [(stage, k) for k in range(n_right + 1) for stage in range(stages)],
        key=lambda step: (step[0] + step[1], step[0]),
    )

    def advance(count=1):
        for _ in range(min(count, len(todo))):
            ring_step(*todo.pop(0))

    advance()

    load_w.wait()
    depth = w_wide.shape[1]

    def part_weights(n, carry):
        at = pl.ds(pl.multiple_of(n * depth, depth), depth)
        block = w_raw[at].astype(F32)
        w_wide[0] = block[:, 0, :]
        w_wide[1] = block[:, 1, :]
        w_ref[0, at, :] = w_wide[0].astype(BF16)
        w_ref[1, at, :] = w_wide[1].astype(BF16)
        return carry

    parts = slab // depth
    lax.fori_loop(0, parts, part_weights, 0)
    advance(2)

    row = lax.broadcasted_iota(jnp.int32, (1, tokens), 1) + ctx * tokens
    keep = retain_ref[...]
    for k in range(starts_ref.shape[1]):
        keep = jnp.where(row == starts_ref[0, k], 0.0, keep)
    mask[...] = jnp.broadcast_to(keep, (LANE, tokens)).T

    lr1 = mod_ref[...] * jnp.cos(phase_ref[...])
    li1 = mod_ref[...] * jnp.sin(phase_ref[...])
    shape = (SEGS, states)
    lr = jnp.broadcast_to(lr1, shape)
    li = jnp.broadcast_to(li1, shape)
    gain = jnp.broadcast_to(gain_ref[...], shape)

    def power(br, bi, n):
        while n > 1:
            br, bi = cmul(br, bi, br, bi)
            n //= 2
        return br, bi

    seg_r, seg_i = power(lr1, li1, steps)
    blk_r, blk_i = power(seg_r, seg_i, SEGS)
    row_r, row_i = power(blk_r, blk_i, nz)

    load_u.wait()
    drive = u_raw[...].astype(F32)
    for j in range(tiles):
        ur[j] = drive[:, 0, lanes_of(j)]
        ui[j] = drive[:, 1, lanes_of(j)]

    def rows(ref, i):
        at = pl.ds(i, SEGS, stride=steps)
        return jnp.concatenate([ref[j, at, :] for j in range(tiles)], axis=1)

    def put_rows(ref, i, value):
        for j in range(tiles):
            ref[j, pl.ds(i, SEGS, stride=steps), :] = value[:, lanes_of(j)]

    def keep_at(i):
        return mask[pl.ds(i, SEGS, stride=steps), :]

    def summary(i, held):
        sr, si, kp = held
        k = keep_at(i)
        kk = wide(k, states)
        tr, ti = cmul(lr, li, sr, si)
        return kk * tr + gain * rows(ur, i), kk * ti + gain * rows(ui, i), kp * k

    zero = jnp.zeros(shape, F32)
    sr, si, kp = lax.fori_loop(0, steps, summary, (zero, zero, jnp.ones((SEGS, LANE), F32)))
    seg[0] = sr
    seg[1] = si
    seg[2] = wide(kp, states)

    def chain(hr, hi, sign, hold):
        order = range(SEGS) if sign > 0 else range(SEGS - 1, -1, -1)
        for g in order:
            if hold is not None:
                hold[0, g:g + 1] = hr
                hold[1, g:g + 1] = hi
            pr, pi = cmul(seg_r, sign * seg_i, hr, hi)
            kg = seg[2, g:g + 1]
            hr = kg * pr + seg[0, g:g + 1]
            hi = kg * pi + seg[1, g:g + 1]
        return hr, hi

    one = jnp.ones((1, states), F32)
    nil = jnp.zeros((1, states), F32)

    def across(buf, mine, n, ar, ai, sign, keeps):
        order = range(n) if sign > 0 else range(n - 1, -1, -1)
        hr, hi, pr, pi, kr = nil, nil, one, nil, one[:, :LANE]
        er, ei, qr, qi = nil, nil, one, nil
        for k in order:
            here = k == mine
            er = jnp.where(here, hr, er)
            ei = jnp.where(here, hi, ei)
            qr = jnp.where(here, pr, qr)
            qi = jnp.where(here, pi, qi)
            kw = wide(keeps[k], states)
            mr, mi = cmul(ar, sign * ai, hr, hi)
            hr = kw * mr + buf[k, :, 0:states]
            hi = kw * mi + buf[k, :, states:2 * states]
            mr, mi = cmul(ar, sign * ai, pr, pi)
            pr, pi = kw * mr, kw * mi
            kr = kr * keeps[k]
        return hr, hi, er, ei, qr, qi, kr

    br, bi = chain(nil, nil, 1, None)
    kb = one[:, :LANE]
    for g in range(SEGS):
        kb = kb * seg[2, g:g + 1, 0:LANE]
    msg_fz[z, :, 0:states] = br
    msg_fz[z, :, states:2 * states] = bi
    msg_fz[z, :, 2 * states:] = kb
    spread(msg_fz, fz_s, fz_r, z, z_peers, at_z)

    for p in y_peers:
        arrived(cslab.at[p], slab_r.at[p])
        for h in range(2):
            ps_send[p, h] = jnp.dot(cslab[p], w_ref[h], preferred_element_type=F32).astype(BF16)
            copy(ps_send.at[p, h], ps_recv.at[y, h], ps_s, ps_r, at_y(p)).start()
    departed(ps_send.at[pl.ds(0, ny - 1)], ps_s)
    advance(2)

    collect(msg_fz, fz_r, z_peers)
    keeps_z = [msg_fz[k, :, 2 * states:] for k in range(nz)]
    hr, hi, er, ei, qr, qi, kx = across(msg_fz, z, nz, blk_r, blk_i, 1, keeps_z)
    msg_fx[x, :, 0:states] = hr
    msg_fx[x, :, states:2 * states] = hi
    msg_fx[x, :, 2 * states:] = kx
    spread(msg_fx, fx_s, fx_r, x, x_peers, at_x)

    advance(2)
    own = cga[z, y]
    for h, ref in ((0, sg_r), (1, sg_i)):
        share = jnp.dot(own, w_ref[h], preferred_element_type=F32)
        for j in range(tiles):
            ref[j] = share[:, lanes_of(j)]
    collect(msg_fx, fx_r, x_peers)
    keeps_x = [msg_fx[k, :, 2 * states:] for k in range(nx)]
    _, _, fr, fi, _, _, _ = across(msg_fx, x, nx, row_r, row_i, 1, keeps_x)
    mr, mi = cmul(qr, qi, fr, fi)
    chain(mr + er, mi + ei, 1, carry_f)

    def fill(i, held):
        sr, si = held
        kk = wide(keep_at(i), states)
        tr, ti = cmul(lr, li, sr, si)
        sr = kk * tr + gain * rows(ur, i)
        si = kk * ti + gain * rows(ui, i)
        put_rows(st_r, i, sr)
        put_rows(st_i, i, si)
        return sr, si

    lax.fori_loop(0, steps, fill, (carry_f[0], carry_f[1]))
    for k in range(nz):
        half[k, :, 0:LANE] = st_r[k].astype(BF16)
        half[k, :, LANE:] = st_i[k].astype(BF16)
    for p in z_peers:
        copy(half.at[p], sga.at[z], sg_s, sg_rs, at_z(p)).start()
    departed(half.at[pl.ds(0, nz - 1)], sg_s)
    sga[z] = half[z]
    advance(2)


    def project(stage):
        count = nz * tokens
        state_t = sga[...].reshape(count, 2 * LANE).T
        for q in range(stage * nc, (stage + 1) * nc):
            block = cga[:, q].reshape(count, slab)
            grad = jnp.dot(state_t, block, preferred_element_type=F32)
            for k in range(nx):
                grads[q, k] = grad[:, lanes_of(k)]
                out_p[q * nx + k] = grad[:, lanes_of(k)].astype(BF16)
                s = copy(out_p.at[q * nx + k], recv_p.at[y * nx + x], p_s, p_r, at_yx(q, k))
                pl.when((q != y) | (k != x))(s.start)

    ring_end(0)
    collect(sga, sg_rs, z_peers)
    project(0)
    advance(len(todo))

    arrived(ps_recv.at[pl.ds(0, ny - 1)], ps_r)
    for p in y_peers:
        for h, ref in ((0, sg_r), (1, sg_i)):
            for j in range(tiles):
                ref[j] += ps_recv[p, h, :, lanes_of(j)].astype(F32)

    def some(ref, i, group):
        at = pl.ds(i, SEGS, stride=steps)
        return jnp.concatenate([ref[j, at, :] for j in group], axis=1)

    def back_step(group, i, held, prior_r, prior_i):
        hr, hi, tr, ti, wr, wi, qr, qi, wg, rr, ri = held
        cols = slice(group[0] * LANE, (group[-1] + 1) * LANE)
        kk = wide(keep_at(i), len(group) * LANE)
        vr, vi = some(ur, i, group), some(ui, i, group)
        xr, xi = some(sg_r, i, group) + hr, some(sg_i, i, group) + hi
        pr, pi = kk * prior_r, kk * prior_i
        wr, wi = wr + (xr * pr + xi * pi), wi + (xi * pr - xr * pi)
        qr, qi = qr + (tr * pr + ti * pi), qi + (ti * pr - tr * pi)
        wg = wg + (xr * vr + xi * vi)
        rr, ri = rr + (tr * vr + ti * vi), ri + (ti * vr - tr * vi)
        ar, ai = kk * lr[:, cols], kk * -li[:, cols]
        hr, hi = cmul(ar, ai, xr, xi)
        tr, ti = cmul(ar, ai, tr, ti)
        return hr, hi, tr, ti, wr, wi, qr, qi, wg, rr, ri

    span = max(1, tiles // 4)
    for first in range(0, tiles, span):
        group = range(first, first + span)
        cols = slice(first * LANE, (first + span) * LANE)
        none = jnp.zeros((SEGS, span * LANE), F32)
        held = (none, none, none + 1.0) + (none,) * 8

        def back(n, held, group=group):
            i = steps - 1 - n
            return back_step(group, i, held, some(st_r, i - 1, group), some(st_i, i - 1, group))

        held = lax.fori_loop(0, steps - 1, back, held)
        held = back_step(group, 0, held, carry_f[0, :, cols], carry_f[1, :, cols])
        for k, value in enumerate(held):
            bseg[k, :, cols] = value

    def fold(held, parts, link):
        hr, hi, pr, pi, wr, wi, qr, qi, wg, rr, ri = held
        br, bi, vr, vi, sr, si, sg, ur_, ui_ = parts
        mr, mi = cmul(sr, si, hr, hi)
        wr, wi = wr + (vr + mr), wi + (vi + mi)
        mr, mi = cmul(sr, si, pr, pi)
        qr, qi = qr + mr, qi + mi
        wg = wg + (sg + (ur_ * hr - ui_ * hi))
        mr, mi = cmul(ur_, ui_, pr, pi)
        rr, ri = rr + mr, ri + mi
        mr, mi = cmul(*link, hr, hi)
        hr, hi = mr + br, mi + bi
        pr, pi = cmul(*link, pr, pi)
        return hr, hi, pr, pi, wr, wi, qr, qi, wg, rr, ri

    fresh = (nil, nil, one) + (nil,) * 8

    def row_of(k, g):
        return bseg[k, g:g + 1]

    held = fresh
    for g in range(SEGS - 1, -1, -1):
        for k in range(4):
            carry_b[k, g:g + 1] = held[k]
        parts = [row_of(k, g) for k in (0, 1, 4, 5, 6, 7, 8, 9, 10)]
        held = fold(held, parts, (row_of(2, g), row_of(3, g)))

    def put(buf, mine, values):
        for k, value in enumerate(values):
            buf[mine, :, k * states:(k + 1) * states] = value

    def join(buf, mine, n, ar, ai, keeps):
        held = fresh
        mark = fresh[:4]
        for k in range(n - 1, -1, -1):
            here = k == mine
            mark = [jnp.where(here, new, old) for new, old in zip(held[:4], mark)]
            kw = wide(keeps[k], states)
            parts = [buf[k, :, m * states:(m + 1) * states] for m in range(9)]
            held = fold(held, parts, (kw * ar, kw * -ai))
        return held, mark

    put(msg_bz, z, held[:2] + held[4:])
    spread(msg_bz, bz_s, bz_r, z, z_peers, at_z)
    for stage in range(1, stages):
        ring_end(stage)
        project(stage)
    collect(msg_bz, bz_r, z_peers)
    held, (er, ei, qr, qi) = join(msg_bz, z, nz, blk_r, blk_i, keeps_z)
    put(msg_bx, x, held[:2] + held[4:])
    spread(msg_bx, bx_s, bx_r, x, x_peers, at_x)
    settle()
    collect(msg_bx, bx_r, x_peers)
    held, (fr, fi, _, _) = join(msg_bx, x, nx, row_r, row_i, keeps_x)
    put(msg_sy, y, (held[4], held[5], held[8]))
    spread(msg_sy, sy_s, sy_r, y, y_peers, at_y)
    mr, mi = cmul(qr, qi, fr, fi)
    mr, mi = cmul(carry_b[2], carry_b[3], mr + er, mi + ei)

    def adjoint(n, held):
        i = steps - 1 - n
        hr, hi = held
        kk = wide(keep_at(i), states)
        ar = rows(sg_r, i) + hr
        ai = rows(sg_i, i) + hi
        put_rows(sg_r, i, gain * ar)
        put_rows(sg_i, i, gain * ai)
        tr, ti = cmul(lr, -li, ar, ai)
        return kk * tr, kk * ti

    lax.fori_loop(0, steps, adjoint, (carry_b[0] + mr, carry_b[1] + mi))
    for h, ref in ((0, sg_r), (1, sg_i)):
        gin_ref[:, h, :] = jnp.concatenate([ref[j].astype(BF16) for j in range(tiles)], axis=1)

    arrived(recv_p.at[pl.ds(0, ny * nx - 1)], p_r)
    departed(out_p.at[pl.ds(0, ny * nx - 1)], p_s)
    grad = grads[y, x]
    for p, q in [(y, q) for q in x_peers] + [(p, x) for p in y_peers] + yx_peers:
        grad = grad + recv_p[p * nx + q].astype(F32)
    out_z[...] = grad.T.reshape(out_z.shape)
    for p in z_peers:
        copy(out_z.at[p], recv_z.at[z], z_s, z_r, at_z(p)).start()
    departed(out_z.at[pl.ds(0, nz - 1)], z_s)
    recv_z[z] = out_z[z]

    collect(msg_sy, sy_r, y_peers)
    sums = msg_sy[0]
    for k in range(1, ny):
        sums = sums + msg_sy[k]
    geig_ref[0:1] = sums[:, 0:states]
    geig_ref[1:2] = sums[:, states:2 * states]
    ggain_ref[...] = sums[:, 2 * states:]

    collect(recv_z, z_r, z_peers)
    for k in range(nz):
        for h in range(2):
            gproj_ref[:, h, lanes_of(k)] = recv_z[k, :, lanes_of(h)]

    settle()


def hand_over(*refs):
    count = len(refs) // 2
    for k in range(count):
        refs[count + k][...] = refs[k][...]


def body(dims, inputs, cotangent, out_proj, modulus, phase, gain, retain, doc_starts, row_blocks):
    ny, nx, nz, nc = dims
    _, tokens, _, states = inputs.shape
    width = cotangent.shape[2]
    slab = width // ny
    stages = ny // nc
    rows_z = LANE // nz
    dma = pltpu.SemaphoreType.DMA

    line = 2 * states + LANE
    scratch = [
        pltpu.VMEM((tokens, 2, states), BF16),
        pltpu.VMEM((tokens, width), BF16),
        pltpu.VMEM((slab, 2, states), BF16),
        pltpu.VMEM((2, LANE, states), F32),
        pltpu.VMEM((2, slab, states), BF16),
        pltpu.VMEM((tokens, LANE), F32),
        *[pltpu.VMEM((states // LANE, tokens, LANE), F32) for _ in range(6)],
        pltpu.VMEM((3, SEGS, states), F32),
        pltpu.VMEM((11, SEGS, states), F32),
        pltpu.VMEM((2, SEGS, states), F32), pltpu.VMEM((4, SEGS, states), F32),
        pltpu.VMEM((nz, ny, tokens, slab), BF16),
        pltpu.VMEM((ny, tokens, slab), BF16),
        pltpu.VMEM((ny, 2, tokens, states), BF16), pltpu.VMEM((ny, 2, tokens, states), BF16),
        pltpu.VMEM((nz, tokens, 2 * LANE), BF16), pltpu.VMEM((nz, tokens, 2 * LANE), BF16),
        pltpu.VMEM((ny, nx, 2 * LANE, LANE), F32),
        pltpu.VMEM((ny * nx, 2 * LANE, LANE), BF16), pltpu.VMEM((ny * nx, 2 * LANE, LANE), BF16),
        pltpu.VMEM((nz, rows_z, 2 * LANE), F32), pltpu.VMEM((nz, rows_z, 2 * LANE), F32),
        pltpu.VMEM((nz, 1, line), F32), pltpu.VMEM((nx, 1, line), F32),
        pltpu.VMEM((nz, 1, 9 * states), F32), pltpu.VMEM((nx, 1, 9 * states), F32),
        pltpu.VMEM((ny, 1, 3 * states), F32),
        dma((3,)), dma, dma((ny,)), dma((stages,)), dma((stages, nz)), dma((stages,)), dma((stages,)),
        *[dma for _ in range(8)],
        *[dma for _ in range(10)],
    ]
    vmem = pl.BlockSpec(memory_space=pltpu.VMEM)
    smem = pl.BlockSpec(memory_space=pltpu.SMEM)
    hbm = pl.BlockSpec(memory_space=pl.ANY)
    results = pl.pallas_call(
        functools.partial(kernel, dims),
        out_shape=(
            jax.ShapeDtypeStruct((tokens, 2, states), BF16),
            jax.ShapeDtypeStruct((rows_z, 2, states), F32),
            jax.ShapeDtypeStruct((2, states), F32),
            jax.ShapeDtypeStruct((1, states), F32),
        ),
        in_specs=[smem, vmem, vmem, vmem, vmem, vmem, hbm, hbm, hbm],
        out_specs=(vmem,) * 4,
        scratch_shapes=scratch,
        compiler_params=pltpu.CompilerParams(
            collective_id=0, has_side_effects=True, vmem_limit_bytes=56 * 1024 * 1024
        ),
    )(
        doc_starts, row_blocks[None], modulus[None], phase[None], gain[None], retain,
        inputs[0], cotangent[0], out_proj,
    )
    grad_inputs, grad_proj, grad_eigen, grad_gain = pl.pallas_call(
        hand_over,
        out_shape=tuple(jax.ShapeDtypeStruct(r.shape, r.dtype) for r in results),
        in_specs=[vmem] * 4,
        out_specs=(vmem,) * 4,
    )(*results)
    return grad_inputs[None], grad_proj, grad_eigen, grad_gain[0]


def solution(mesh):
    sizes = mesh.shape
    nx, nz = grid_of(sizes["ctx"])
    dims = (sizes["dp"], nx, nz, sizes["chan"])
    return jax.shard_map(
        functools.partial(body, dims),
        mesh=mesh,
        in_specs=(
            P("dp", "ctx", None, "chan"),
            P("dp", "ctx", None),
            P("dp", None, "chan"),
            P("chan"),
            P("chan"),
            P("chan"),
            P("dp", "ctx"),
            P("dp", None),
            P("dp"),
        ),
        out_specs=(
            P("dp", "ctx", None, "chan"),
            P(("dp", "ctx"), None, "chan"),
            P(None, "chan"),
            P("chan"),
        ),
        check_vma=False,
    )
```

```python
import functools

import jax
import jax.numpy as jnp
from jax import lax
from jax.experimental import pallas as pl
from jax.experimental.pallas import tpu as pltpu
from jax.sharding import PartitionSpec as P

MESH = pl.DeviceIdType.MESH
F32 = jnp.float32
BF16 = jnp.bfloat16
LANE = 128
SEGS = 8


def grid_of(ctx):
    z = {32: 8, 4: 2, 8: 4}[ctx]
    return ctx // z, z


def cmul(ar, ai, br, bi):
    return ar * br - ai * bi, ar * bi + ai * br


def wide(row, states):
    return jnp.concatenate([row] * (states // LANE), axis=1)


def lanes_of(j):
    return slice(j * LANE, (j + 1) * LANE)


def nearest_last(n):
    return sorted(range(1, n), key=lambda k: -min(k, n - k))


def kernel(
    dims,
    starts_ref, blocks_ref, mod_ref, phase_ref, gain_ref, retain_ref, u_hbm, cot_hbm, w_hbm,
    gin_ref, gproj_ref, geig_ref, ggain_ref,
    u_raw, cot_raw, w_raw, w_wide, w_ref, mask,
    ur, ui, st_r, st_i, sg_r, sg_i, seg, bseg, carry_f, carry_b,
    cga, cslab, ps_send, ps_recv, half, sga, state_t, grads, out_x, recv_x, out_y, recv_y, out_z, recv_z,
    msg_fz, msg_fx, msg_bz, msg_bx, msg_sy,
    load_s, slab_s, slab_r, ag_s, ag_r, dd_s, dd_r, ps_s, ps_r, sg_s, sg_rs,
    x_s, x_r, y_s, y_r, z_s, z_r,
    fz_s, fz_r, fx_s, fx_r, bz_s, bz_r, bx_s, bx_r, sy_s, sy_r,
):
    ny, nx, nz, nc = dims
    tokens, width = cot_raw.shape
    tiles = ur.shape[0]
    states = tiles * LANE
    steps = tokens // SEGS
    slab = width // ny
    stages = ny // nc
    y = lax.axis_index("dp")
    ctx = lax.axis_index("ctx")
    c = lax.axis_index("chan")
    x, z = ctx // nz, ctx % nz

    def at_z(other):
        return (y, x * nz + other, c)

    def at_x(other):
        return (y, other * nz + z, c)

    def at_y(other):
        return (other, ctx, c)

    sibling = (y, ctx, 1 - c)
    z_peers = [(z + k) % nz for k in nearest_last(nz)]
    x_peers = [(x + k) % nx for k in nearest_last(nx)]
    y_peers = [(y + k) % ny for k in nearest_last(ny)]

    def copy(src, dst, ssem, rsem, device):
        return pltpu.make_async_remote_copy(
            src_ref=src, dst_ref=dst, send_sem=ssem, recv_sem=rsem,
            device_id=device, device_id_type=MESH,
        )

    barrier = pltpu.get_barrier_semaphore()
    greeted = [at_z(p) for p in z_peers] + [at_x(p) for p in x_peers]
    greeted += [at_y(p) for p in y_peers] + [sibling]
    for device in greeted:
        pl.semaphore_signal(barrier, inc=1, device_id=device, device_id_type=MESH)
    load_cot = pltpu.make_async_copy(cot_hbm, cot_raw, load_s.at[0])
    load_u = pltpu.make_async_copy(u_hbm, u_raw, load_s.at[1])
    load_w = pltpu.make_async_copy(w_hbm, w_raw, load_s.at[2])
    load_cot.start()
    load_u.start()
    load_w.start()

    alive = jnp.where(ctx < blocks_ref[...], 1.0, 0.0)
    alive = jnp.broadcast_to(alive, (tokens, slab)).astype(BF16)
    load_cot.wait()
    for q in range(ny):
        cga[z, q] = cot_raw[:, q * slab:(q + 1) * slab] * alive
    pl.semaphore_wait(barrier, len(greeted))

    def arrived(view, rsem):
        copy(view, view, rsem, rsem, sibling).wait_recv()

    def departed(view, ssem):
        pending.append(copy(view, view, ssem, ssem, sibling))

    def settle():
        for s in pending:
            s.wait_send()
        pending.clear()

    def spread(buf, ssem, rsem, mine, peers, where):
        for p in peers:
            copy(buf.at[mine], buf.at[mine], ssem, rsem, where(p)).start()
        if peers:
            departed(buf.at[pl.ds(0, len(peers))], ssem)

    def collect(buf, rsem, peers):
        if peers:
            arrived(buf.at[pl.ds(0, len(peers))], rsem)

    pending = []

    for p in y_peers:
        copy(cga.at[z, p], cslab.at[y], slab_s, slab_r.at[y], at_y(p)).start()
    departed(cslab.at[pl.ds(0, ny - 1)], slab_s)

    hops = nz // 2
    split = tokens // 2

    def ring_part(slot, q, k, way):
        if k < hops or nz % 2:
            return cga.at[slot, q]
        return cga.at[slot, q, pl.ds(way * split, split)]

    def ring_step(stage, k):
        q = stage * nc + c
        for way in range(2):
            sign = -1 if way == 0 else 1
            slot = (z + sign * k) % nz
            if k >= 1:
                arrived(ring_part(slot, q, k, way), ag_r.at[stage, way, k])
            if k < hops:
                part = ring_part(slot, q, k + 1, way)
                to = at_z((z - sign) % nz)
                copy(part, part, ag_s.at[stage], ag_r.at[stage, way, k + 1], to).start()
            if k >= 1:
                part = ring_part(slot, q, k, way)
                copy(part, part, dd_s.at[stage], dd_r.at[stage], sibling).start()
        if k == hops:
            departed(cga.at[pl.ds(0, nz - 1), q], ag_s.at[stage])
            departed(cga.at[pl.ds(0, nz - 1), q], dd_s.at[stage])

    def ring_end(stage):
        arrived(cga.at[pl.ds(0, nz - 1), stage * nc + 1 - c], dd_r.at[stage])

    todo = sorted(
        [(stage, k) for k in range(hops + 1) for stage in range(stages)],
        key=lambda step: (step[0] + step[1], step[0]),
    )

    def advance(count=1):
        for _ in range(min(count, len(todo))):
            ring_step(*todo.pop(0))

    advance()

    row = lax.broadcasted_iota(jnp.int32, (1, tokens), 1) + ctx * tokens
    keep = retain_ref[...]
    for k in range(starts_ref.shape[1]):
        keep = jnp.where(row == starts_ref[0, k], 0.0, keep)
    mask[...] = jnp.broadcast_to(keep, (LANE, tokens)).T

    lr1 = mod_ref[...] * jnp.cos(phase_ref[...])
    li1 = mod_ref[...] * jnp.sin(phase_ref[...])
    shape = (SEGS, states)
    lr = jnp.broadcast_to(lr1, shape)
    li = jnp.broadcast_to(li1, shape)
    gain = jnp.broadcast_to(gain_ref[...], shape)

    def power(br, bi, n):
        while n > 1:
            br, bi = cmul(br, bi, br, bi)
            n //= 2
        return br, bi

    seg_r, seg_i = power(lr1, li1, steps)
    blk_r, blk_i = power(seg_r, seg_i, SEGS)
    row_r, row_i = power(blk_r, blk_i, nz)

    load_u.wait()
    drive = u_raw[...].astype(F32)
    for j in range(tiles):
        ur[j] = drive[:, 0, lanes_of(j)]
        ui[j] = drive[:, 1, lanes_of(j)]

    def rows(ref, i):
        at = pl.ds(i, SEGS, stride=steps)
        return jnp.concatenate([ref[j, at, :] for j in range(tiles)], axis=1)

    def put_rows(ref, i, value):
        for j in range(tiles):
            ref[j, pl.ds(i, SEGS, stride=steps), :] = value[:, lanes_of(j)]

    def keep_at(i):
        return mask[pl.ds(i, SEGS, stride=steps), :]

    def summary(i, held):
        sr, si, kp = held
        k = keep_at(i)
        kk = wide(k, states)
        tr, ti = cmul(lr, li, sr, si)
        return kk * tr + gain * rows(ur, i), kk * ti + gain * rows(ui, i), kp * k

    zero = jnp.zeros(shape, F32)
    sr, si, kp = lax.fori_loop(0, steps, summary, (zero, zero, jnp.ones((SEGS, LANE), F32)))
    seg[0] = sr
    seg[1] = si
    seg[2] = wide(kp, states)

    def chain(hr, hi, sign, hold):
        order = range(SEGS) if sign > 0 else range(SEGS - 1, -1, -1)
        for g in order:
            if hold is not None:
                hold[0, g:g + 1] = hr
                hold[1, g:g + 1] = hi
            pr, pi = cmul(seg_r, sign * seg_i, hr, hi)
            kg = seg[2, g:g + 1]
            hr = kg * pr + seg[0, g:g + 1]
            hi = kg * pi + seg[1, g:g + 1]
        return hr, hi

    one = jnp.ones((1, states), F32)
    nil = jnp.zeros((1, states), F32)

    def across(buf, mine, n, ar, ai, sign, keeps):
        order = range(n) if sign > 0 else range(n - 1, -1, -1)
        hr, hi, pr, pi, kr = nil, nil, one, nil, one[:, :LANE]
        er, ei, qr, qi = nil, nil, one, nil
        for k in order:
            here = k == mine
            er = jnp.where(here, hr, er)
            ei = jnp.where(here, hi, ei)
            qr = jnp.where(here, pr, qr)
            qi = jnp.where(here, pi, qi)
            kw = wide(keeps[k], states)
            mr, mi = cmul(ar, sign * ai, hr, hi)
            hr = kw * mr + buf[k, :, 0:states]
            hi = kw * mi + buf[k, :, states:2 * states]
            mr, mi = cmul(ar, sign * ai, pr, pi)
            pr, pi = kw * mr, kw * mi
            kr = kr * keeps[k]
        return hr, hi, er, ei, qr, qi, kr

    br, bi = chain(nil, nil, 1, None)
    kb = one[:, :LANE]
    for g in range(SEGS):
        kb = kb * seg[2, g:g + 1, 0:LANE]
    msg_fz[z, :, 0:states] = br
    msg_fz[z, :, states:2 * states] = bi
    msg_fz[z, :, 2 * states:] = kb
    spread(msg_fz, fz_s, fz_r, z, z_peers, at_z)

    advance(2)
    load_w.wait()
    depth = w_wide.shape[1]

    def part_weights(n, carry):
        at = pl.ds(pl.multiple_of(n * depth, depth), depth)
        block = w_raw[at].astype(F32)
        w_wide[0] = block[:, 0, :]
        w_wide[1] = block[:, 1, :]
        w_ref[0, at, :] = w_wide[0].astype(BF16)
        w_ref[1, at, :] = w_wide[1].astype(BF16)
        return carry

    parts = slab // depth
    lax.fori_loop(0, parts, part_weights, 0)

    for p in y_peers:
        arrived(cslab.at[p], slab_r.at[p])
        for h in range(2):
            ps_send[p, h] = jnp.dot(cslab[p], w_ref[h], preferred_element_type=F32).astype(BF16)
            copy(ps_send.at[p, h], ps_recv.at[y, h], ps_s, ps_r, at_y(p)).start()
    departed(ps_send.at[pl.ds(0, ny - 1)], ps_s)
    advance(2)

    collect(msg_fz, fz_r, z_peers)
    keeps_z = [msg_fz[k, :, 2 * states:] for k in range(nz)]
    hr, hi, er, ei, qr, qi, kx = across(msg_fz, z, nz, blk_r, blk_i, 1, keeps_z)
    msg_fx[x, :, 0:states] = hr
    msg_fx[x, :, states:2 * states] = hi
    msg_fx[x, :, 2 * states:] = kx
    spread(msg_fx, fx_s, fx_r, x, x_peers, at_x)

    advance(2)
    own = cga[z, y]
    for h, ref in ((0, sg_r), (1, sg_i)):
        share = jnp.dot(own, w_ref[h], preferred_element_type=F32)
        for j in range(tiles):
            ref[j] = share[:, lanes_of(j)]
    collect(msg_fx, fx_r, x_peers)
    keeps_x = [msg_fx[k, :, 2 * states:] for k in range(nx)]
    _, _, fr, fi, _, _, _ = across(msg_fx, x, nx, row_r, row_i, 1, keeps_x)
    mr, mi = cmul(qr, qi, fr, fi)
    chain(mr + er, mi + ei, 1, carry_f)

    def fill(i, held):
        sr, si = held
        kk = wide(keep_at(i), states)
        tr, ti = cmul(lr, li, sr, si)
        sr = kk * tr + gain * rows(ur, i)
        si = kk * ti + gain * rows(ui, i)
        put_rows(st_r, i, sr)
        put_rows(st_i, i, si)
        return sr, si

    lax.fori_loop(0, steps, fill, (carry_f[0], carry_f[1]))
    for k in range(nz):
        half[k, :, 0:LANE] = st_r[k].astype(BF16)
        half[k, :, LANE:] = st_i[k].astype(BF16)
    for p in z_peers:
        copy(half.at[p], sga.at[z], sg_s, sg_rs, at_z(p)).start()
    departed(half.at[pl.ds(0, nz - 1)], sg_s)
    sga[z] = half[z]
    advance(2)


    def project(stage):
        count = nz * tokens
        if stage == 0:
            state_t[...] = sga[...].reshape(count, 2 * LANE).T
        for q in range(stage * nc, (stage + 1) * nc):
            block = cga[:, q].reshape(count, slab)
            grad = jnp.dot(state_t[...], block, preferred_element_type=F32)
            for k in range(nx):
                grads[q, k] = grad[:, lanes_of(k)]
                out_x[k, q] = grad[:, lanes_of(k)].astype(BF16)
            for p in x_peers:
                copy(out_x.at[p, q], recv_x.at[x, q], x_s, x_r, at_x(p)).start()

    ring_end(0)
    collect(sga, sg_rs, z_peers)
    project(0)
    advance(len(todo))

    arrived(ps_recv.at[pl.ds(0, ny - 1)], ps_r)
    for p in y_peers:
        for h, ref in ((0, sg_r), (1, sg_i)):
            for j in range(tiles):
                ref[j] += ps_recv[p, h, :, lanes_of(j)].astype(F32)

    def some(ref, i, group):
        at = pl.ds(i, SEGS, stride=steps)
        return jnp.concatenate([ref[j, at, :] for j in group], axis=1)

    def back_step(group, i, held, prior_r, prior_i):
        hr, hi, tr, ti, wr, wi, qr, qi, wg, rr, ri = held
        cols = slice(group[0] * LANE, (group[-1] + 1) * LANE)
        kk = wide(keep_at(i), len(group) * LANE)
        vr, vi = some(ur, i, group), some(ui, i, group)
        xr, xi = some(sg_r, i, group) + hr, some(sg_i, i, group) + hi
        pr, pi = kk * prior_r, kk * prior_i
        wr, wi = wr + (xr * pr + xi * pi), wi + (xi * pr - xr * pi)
        qr, qi = qr + (tr * pr + ti * pi), qi + (ti * pr - tr * pi)
        wg = wg + (xr * vr + xi * vi)
        rr, ri = rr + (tr * vr + ti * vi), ri + (ti * vr - tr * vi)
        ar, ai = kk * lr[:, cols], kk * -li[:, cols]
        hr, hi = cmul(ar, ai, xr, xi)
        tr, ti = cmul(ar, ai, tr, ti)
        return hr, hi, tr, ti, wr, wi, qr, qi, wg, rr, ri

    span = max(1, tiles // 4)
    for first in range(0, tiles, span):
        group = range(first, first + span)
        cols = slice(first * LANE, (first + span) * LANE)
        none = jnp.zeros((SEGS, span * LANE), F32)
        held = (none, none, none + 1.0) + (none,) * 8

        def back(n, held, group=group):
            i = steps - 1 - n
            return back_step(group, i, held, some(st_r, i - 1, group), some(st_i, i - 1, group))

        held = lax.fori_loop(0, steps - 1, back, held)
        held = back_step(group, 0, held, carry_f[0, :, cols], carry_f[1, :, cols])
        for k, value in enumerate(held):
            bseg[k, :, cols] = value

    def fold(held, parts, link):
        hr, hi, pr, pi, wr, wi, qr, qi, wg, rr, ri = held
        br, bi, vr, vi, sr, si, sg, ur_, ui_ = parts
        mr, mi = cmul(sr, si, hr, hi)
        wr, wi = wr + (vr + mr), wi + (vi + mi)
        mr, mi = cmul(sr, si, pr, pi)
        qr, qi = qr + mr, qi + mi
        wg = wg + (sg + (ur_ * hr - ui_ * hi))
        mr, mi = cmul(ur_, ui_, pr, pi)
        rr, ri = rr + mr, ri + mi
        mr, mi = cmul(*link, hr, hi)
        hr, hi = mr + br, mi + bi
        pr, pi = cmul(*link, pr, pi)
        return hr, hi, pr, pi, wr, wi, qr, qi, wg, rr, ri

    fresh = (nil, nil, one) + (nil,) * 8

    def row_of(k, g):
        return bseg[k, g:g + 1]

    held = fresh
    for g in range(SEGS - 1, -1, -1):
        for k in range(4):
            carry_b[k, g:g + 1] = held[k]
        parts = [row_of(k, g) for k in (0, 1, 4, 5, 6, 7, 8, 9, 10)]
        held = fold(held, parts, (row_of(2, g), row_of(3, g)))

    def put(buf, mine, values):
        for k, value in enumerate(values):
            buf[mine, :, k * states:(k + 1) * states] = value

    def join(buf, mine, n, ar, ai, keeps):
        held = fresh
        mark = fresh[:4]
        for k in range(n - 1, -1, -1):
            here = k == mine
            mark = [jnp.where(here, new, old) for new, old in zip(held[:4], mark)]
            kw = wide(keeps[k], states)
            parts = [buf[k, :, m * states:(m + 1) * states] for m in range(9)]
            held = fold(held, parts, (kw * ar, kw * -ai))
        return held, mark

    put(msg_bz, z, held[:2] + held[4:])
    spread(msg_bz, bz_s, bz_r, z, z_peers, at_z)
    for stage in range(1, stages):
        ring_end(stage)
        project(stage)
    collect(msg_bz, bz_r, z_peers)
    held, (er, ei, qr, qi) = join(msg_bz, z, nz, blk_r, blk_i, keeps_z)
    put(msg_bx, x, held[:2] + held[4:])
    spread(msg_bx, bx_s, bx_r, x, x_peers, at_x)
    if nx > 1:
        arrived(recv_x.at[pl.ds(0, nx - 1)], x_r)
        departed(out_x.at[pl.ds(0, nx - 1)], x_s)
    for q in range(ny):
        grad = grads[q, x]
        for p in x_peers:
            grad = grad + recv_x[p, q].astype(F32)
        grads[q, 0] = grad
        out_y[q] = grad.astype(BF16)
    for p in y_peers:
        copy(out_y.at[p], recv_y.at[y], y_s, y_r, at_y(p)).start()
    settle()
    collect(msg_bx, bx_r, x_peers)
    held, (fr, fi, _, _) = join(msg_bx, x, nx, row_r, row_i, keeps_x)
    put(msg_sy, y, (held[4], held[5], held[8]))
    spread(msg_sy, sy_s, sy_r, y, y_peers, at_y)
    mr, mi = cmul(qr, qi, fr, fi)
    mr, mi = cmul(carry_b[2], carry_b[3], mr + er, mi + ei)

    def adjoint(n, held):
        i = steps - 1 - n
        hr, hi = held
        kk = wide(keep_at(i), states)
        ar = rows(sg_r, i) + hr
        ai = rows(sg_i, i) + hi
        put_rows(sg_r, i, gain * ar)
        put_rows(sg_i, i, gain * ai)
        tr, ti = cmul(lr, -li, ar, ai)
        return kk * tr, kk * ti

    lax.fori_loop(0, steps, adjoint, (carry_b[0] + mr, carry_b[1] + mi))
    for h, ref in ((0, sg_r), (1, sg_i)):
        gin_ref[:, h, :] = jnp.concatenate([ref[j].astype(BF16) for j in range(tiles)], axis=1)

    if ny > 1:
        arrived(recv_y.at[pl.ds(0, ny - 1)], y_r)
        departed(out_y.at[pl.ds(0, ny - 1)], y_s)
    grad = grads[y, 0]
    for p in y_peers:
        grad = grad + recv_y[p].astype(F32)
    out_z[...] = grad.T.reshape(out_z.shape)
    for p in z_peers:
        copy(out_z.at[p], recv_z.at[z], z_s, z_r, at_z(p)).start()
    departed(out_z.at[pl.ds(0, nz - 1)], z_s)
    recv_z[z] = out_z[z]

    collect(msg_sy, sy_r, y_peers)
    sums = msg_sy[0]
    for k in range(1, ny):
        sums = sums + msg_sy[k]
    geig_ref[0:1] = sums[:, 0:states]
    geig_ref[1:2] = sums[:, states:2 * states]
    ggain_ref[...] = sums[:, 2 * states:]

    collect(recv_z, z_r, z_peers)
    for k in range(nz):
        for h in range(2):
            gproj_ref[:, h, lanes_of(k)] = recv_z[k, :, lanes_of(h)]

    settle()


def hand_over(*refs):
    count = len(refs) // 2
    for k in range(count):
        refs[count + k][...] = refs[k][...]


def body(dims, inputs, cotangent, out_proj, modulus, phase, gain, retain, doc_starts, row_blocks):
    ny, nx, nz, nc = dims
    _, tokens, _, states = inputs.shape
    width = cotangent.shape[2]
    slab = width // ny
    stages = ny // nc
    rows_z = LANE // nz
    dma = pltpu.SemaphoreType.DMA

    line = 2 * states + LANE
    scratch = [
        pltpu.VMEM((tokens, 2, states), BF16),
        pltpu.VMEM((tokens, width), BF16),
        pltpu.VMEM((slab, 2, states), BF16),
        pltpu.VMEM((2, LANE, states), F32),
        pltpu.VMEM((2, slab, states), BF16),
        pltpu.VMEM((tokens, LANE), F32),
        *[pltpu.VMEM((states // LANE, tokens, LANE), F32) for _ in range(6)],
        pltpu.VMEM((3, SEGS, states), F32),
        pltpu.VMEM((11, SEGS, states), F32),
        pltpu.VMEM((2, SEGS, states), F32), pltpu.VMEM((4, SEGS, states), F32),
        pltpu.VMEM((nz, ny, tokens, slab), BF16),
        pltpu.VMEM((ny, tokens, slab), BF16),
        pltpu.VMEM((ny, 2, tokens, states), BF16), pltpu.VMEM((ny, 2, tokens, states), BF16),
        pltpu.VMEM((nz, tokens, 2 * LANE), BF16), pltpu.VMEM((nz, tokens, 2 * LANE), BF16),
        pltpu.VMEM((2 * LANE, nz * tokens), BF16),
        pltpu.VMEM((ny, nx, 2 * LANE, LANE), F32),
        pltpu.VMEM((nx, ny, 2 * LANE, LANE), BF16), pltpu.VMEM((nx, ny, 2 * LANE, LANE), BF16),
        pltpu.VMEM((ny, 2 * LANE, LANE), BF16), pltpu.VMEM((ny, 2 * LANE, LANE), BF16),
        pltpu.VMEM((nz, rows_z, 2 * LANE), F32), pltpu.VMEM((nz, rows_z, 2 * LANE), F32),
        pltpu.VMEM((nz, 1, line), F32), pltpu.VMEM((nx, 1, line), F32),
        pltpu.VMEM((nz, 1, 9 * states), F32), pltpu.VMEM((nx, 1, 9 * states), F32),
        pltpu.VMEM((ny, 1, 3 * states), F32),
        dma((3,)), dma, dma((ny,)), dma((stages,)), dma((stages, 2, nz)), dma((stages,)), dma((stages,)),
        *[dma for _ in range(10)],
        *[dma for _ in range(10)],
    ]
    vmem = pl.BlockSpec(memory_space=pltpu.VMEM)
    smem = pl.BlockSpec(memory_space=pltpu.SMEM)
    hbm = pl.BlockSpec(memory_space=pl.ANY)
    results = pl.pallas_call(
        functools.partial(kernel, dims),
        out_shape=(
            jax.ShapeDtypeStruct((tokens, 2, states), BF16),
            jax.ShapeDtypeStruct((rows_z, 2, states), F32),
            jax.ShapeDtypeStruct((2, states), F32),
            jax.ShapeDtypeStruct((1, states), F32),
        ),
        in_specs=[smem, vmem, vmem, vmem, vmem, vmem, hbm, hbm, hbm],
        out_specs=(vmem,) * 4,
        scratch_shapes=scratch,
        compiler_params=pltpu.CompilerParams(
            collective_id=0, has_side_effects=True, vmem_limit_bytes=56 * 1024 * 1024
        ),
    )(
        doc_starts, row_blocks[None], modulus[None], phase[None], gain[None], retain,
        inputs[0], cotangent[0], out_proj,
    )
    grad_inputs, grad_proj, grad_eigen, grad_gain = pl.pallas_call(
        hand_over,
        out_shape=tuple(jax.ShapeDtypeStruct(r.shape, r.dtype) for r in results),
        in_specs=[vmem] * 4,
        out_specs=(vmem,) * 4,
    )(*results)
    return grad_inputs[None], grad_proj, grad_eigen, grad_gain[0]


def solution(mesh):
    sizes = mesh.shape
    nx, nz = grid_of(sizes["ctx"])
    dims = (sizes["dp"], nx, nz, sizes["chan"])
    return jax.shard_map(
        functools.partial(body, dims),
        mesh=mesh,
        in_specs=(
            P("dp", "ctx", None, "chan"),
            P("dp", "ctx", None),
            P("dp", None, "chan"),
            P("chan"),
            P("chan"),
            P("chan"),
            P("dp", "ctx"),
            P("dp", None),
            P("dp"),
        ),
        out_specs=(
            P("dp", "ctx", None, "chan"),
            P(("dp", "ctx"), None, "chan"),
            P(None, "chan"),
            P("chan"),
        ),
        check_vma=False,
    )
```

```python
import functools

import jax
import jax.numpy as jnp
from jax import lax
from jax.experimental import pallas as pl
from jax.experimental.pallas import tpu as pltpu
from jax.sharding import PartitionSpec as P

MESH = pl.DeviceIdType.MESH
F32 = jnp.float32
BF16 = jnp.bfloat16
LANE = 128
SEGS = 8


def grid_of(ctx):
    z = {32: 8, 4: 2, 8: 4}[ctx]
    return ctx // z, z


def cmul(ar, ai, br, bi):
    return ar * br - ai * bi, ar * bi + ai * br


def wide(row, states):
    return jnp.concatenate([row] * (states // LANE), axis=1)


def lanes_of(j):
    return slice(j * LANE, (j + 1) * LANE)


def nearest_last(n):
    return sorted(range(1, n), key=lambda k: -min(k, n - k))


def kernel(
    dims,
    starts_ref, blocks_ref, mod_ref, phase_ref, gain_ref, retain_ref, u_hbm, cot_hbm, w_hbm,
    gin_ref, gproj_ref, geig_ref, ggain_ref,
    gin_raw, u_raw, cot_raw, w_raw, w_wide, w_ref, mask,
    ur, ui, st_r, st_i, sg_r, sg_i, seg, bseg, carry_f, carry_b,
    cga, cslab, ps_send, ps_recv, half, sga, state_t, grads, out_x, recv_x, out_y, recv_y, out_z, recv_z,
    msg_fz, msg_fx, msg_bz, msg_bx, msg_sy,
    load_s, slab_s, slab_r, ag_s, ag_r, dd_s, dd_r, ps_s, ps_r, sg_s, sg_rs,
    x_s, x_r, y_s, y_r, z_s, z_r,
    fz_s, fz_r, fx_s, fx_r, bz_s, bz_r, bx_s, bx_r, sy_s, sy_r,
):
    ny, nx, nz, nc = dims
    tokens, width = cot_raw.shape
    tiles = ur.shape[0]
    states = tiles * LANE
    steps = tokens // SEGS
    slab = width // ny
    stages = ny // nc
    y = lax.axis_index("dp")
    ctx = lax.axis_index("ctx")
    c = lax.axis_index("chan")
    x, z = ctx // nz, ctx % nz

    def at_z(other):
        return (y, x * nz + other, c)

    def at_x(other):
        return (y, other * nz + z, c)

    def at_y(other):
        return (other, ctx, c)

    sibling = (y, ctx, 1 - c)
    z_peers = [(z + k) % nz for k in nearest_last(nz)]
    x_peers = [(x + k) % nx for k in nearest_last(nx)]
    y_peers = [(y + k) % ny for k in nearest_last(ny)]

    def copy(src, dst, ssem, rsem, device):
        return pltpu.make_async_remote_copy(
            src_ref=src, dst_ref=dst, send_sem=ssem, recv_sem=rsem,
            device_id=device, device_id_type=MESH,
        )

    barrier = pltpu.get_barrier_semaphore()
    greeted = [at_z(p) for p in z_peers] + [at_x(p) for p in x_peers]
    greeted += [at_y(p) for p in y_peers] + [sibling]
    for device in greeted:
        pl.semaphore_signal(barrier, inc=1, device_id=device, device_id_type=MESH)
    load_cot = pltpu.make_async_copy(cot_hbm, cot_raw, load_s.at[0])
    load_u = pltpu.make_async_copy(u_hbm, u_raw, load_s.at[1])
    load_w = pltpu.make_async_copy(w_hbm, w_raw, load_s.at[2])
    load_cot.start()
    load_u.start()
    load_w.start()

    alive = jnp.where(ctx < blocks_ref[...], 1.0, 0.0)
    alive = jnp.broadcast_to(alive, (tokens, slab)).astype(BF16)
    load_cot.wait()
    for q in range(ny):
        cga[z, q] = cot_raw[:, q * slab:(q + 1) * slab] * alive
    pl.semaphore_wait(barrier, len(greeted))

    def arrived(view, rsem):
        copy(view, view, rsem, rsem, sibling).wait_recv()

    def departed(view, ssem):
        pending.append(copy(view, view, ssem, ssem, sibling))

    def settle():
        for s in pending:
            s.wait_send()
        pending.clear()

    def spread(buf, ssem, rsem, mine, peers, where):
        for p in peers:
            copy(buf.at[mine], buf.at[mine], ssem, rsem, where(p)).start()
        if peers:
            departed(buf.at[pl.ds(0, len(peers))], ssem)

    def collect(buf, rsem, peers):
        if peers:
            arrived(buf.at[pl.ds(0, len(peers))], rsem)

    pending = []

    for p in y_peers:
        copy(cga.at[z, p], cslab.at[y], slab_s, slab_r.at[y], at_y(p)).start()
    departed(cslab.at[pl.ds(0, ny - 1)], slab_s)

    hops = nz // 2
    split = tokens // 2

    def ring_part(slot, q, k, way):
        if k < hops or nz % 2:
            return cga.at[slot, q]
        return cga.at[slot, q, pl.ds(way * split, split)]

    def ring_step(stage, k):
        q = stage * nc + c
        for way in range(2):
            sign = -1 if way == 0 else 1
            slot = (z + sign * k) % nz
            if k >= 1:
                arrived(ring_part(slot, q, k, way), ag_r.at[stage, way, k])
            if k < hops:
                part = ring_part(slot, q, k + 1, way)
                to = at_z((z - sign) % nz)
                copy(part, part, ag_s.at[stage], ag_r.at[stage, way, k + 1], to).start()
            if k >= 1:
                part = ring_part(slot, q, k, way)
                copy(part, part, dd_s.at[stage], dd_r.at[stage], sibling).start()
        if k == hops:
            departed(cga.at[pl.ds(0, nz - 1), q], ag_s.at[stage])
            departed(cga.at[pl.ds(0, nz - 1), q], dd_s.at[stage])

    def ring_end(stage):
        arrived(cga.at[pl.ds(0, nz - 1), stage * nc + 1 - c], dd_r.at[stage])

    todo = sorted(
        [(stage, k) for k in range(hops + 1) for stage in range(stages)],
        key=lambda step: (step[0] + step[1], step[0]),
    )

    def advance(count=1):
        for _ in range(min(count, len(todo))):
            ring_step(*todo.pop(0))

    advance()

    row = lax.broadcasted_iota(jnp.int32, (1, tokens), 1) + ctx * tokens
    keep = retain_ref[...]
    for k in range(starts_ref.shape[1]):
        keep = jnp.where(row == starts_ref[0, k], 0.0, keep)
    mask[...] = jnp.broadcast_to(keep, (LANE, tokens)).T

    lr1 = mod_ref[...] * jnp.cos(phase_ref[...])
    li1 = mod_ref[...] * jnp.sin(phase_ref[...])
    shape = (SEGS, states)
    lr = jnp.broadcast_to(lr1, shape)
    li = jnp.broadcast_to(li1, shape)
    gain = jnp.broadcast_to(gain_ref[...], shape)

    def power(br, bi, n):
        while n > 1:
            br, bi = cmul(br, bi, br, bi)
            n //= 2
        return br, bi

    seg_r, seg_i = power(lr1, li1, steps)
    blk_r, blk_i = power(seg_r, seg_i, SEGS)
    row_r, row_i = power(blk_r, blk_i, nz)

    load_u.wait()
    drive = u_raw[...].astype(F32)
    for j in range(tiles):
        ur[j] = drive[:, 0, lanes_of(j)]
        ui[j] = drive[:, 1, lanes_of(j)]

    def rows(ref, i):
        at = pl.ds(i, SEGS, stride=steps)
        return jnp.concatenate([ref[j, at, :] for j in range(tiles)], axis=1)

    def put_rows(ref, i, value):
        for j in range(tiles):
            ref[j, pl.ds(i, SEGS, stride=steps), :] = value[:, lanes_of(j)]

    def keep_at(i):
        return mask[pl.ds(i, SEGS, stride=steps), :]

    def summary(i, held):
        sr, si, kp = held
        k = keep_at(i)
        kk = wide(k, states)
        tr, ti = cmul(lr, li, sr, si)
        return kk * tr + gain * rows(ur, i), kk * ti + gain * rows(ui, i), kp * k

    zero = jnp.zeros(shape, F32)
    sr, si, kp = lax.fori_loop(0, steps, summary, (zero, zero, jnp.ones((SEGS, LANE), F32)))
    seg[0] = sr
    seg[1] = si
    seg[2] = wide(kp, states)

    def chain(hr, hi, sign, hold):
        order = range(SEGS) if sign > 0 else range(SEGS - 1, -1, -1)
        for g in order:
            if hold is not None:
                hold[0, g:g + 1] = hr
                hold[1, g:g + 1] = hi
            pr, pi = cmul(seg_r, sign * seg_i, hr, hi)
            kg = seg[2, g:g + 1]
            hr = kg * pr + seg[0, g:g + 1]
            hi = kg * pi + seg[1, g:g + 1]
        return hr, hi

    one = jnp.ones((1, states), F32)
    nil = jnp.zeros((1, states), F32)

    def across(buf, mine, n, ar, ai, sign, keeps):
        order = range(n) if sign > 0 else range(n - 1, -1, -1)
        hr, hi, pr, pi, kr = nil, nil, one, nil, one[:, :LANE]
        er, ei, qr, qi = nil, nil, one, nil
        for k in order:
            here = k == mine
            er = jnp.where(here, hr, er)
            ei = jnp.where(here, hi, ei)
            qr = jnp.where(here, pr, qr)
            qi = jnp.where(here, pi, qi)
            kw = wide(keeps[k], states)
            mr, mi = cmul(ar, sign * ai, hr, hi)
            hr = kw * mr + buf[k, :, 0:states]
            hi = kw * mi + buf[k, :, states:2 * states]
            mr, mi = cmul(ar, sign * ai, pr, pi)
            pr, pi = kw * mr, kw * mi
            kr = kr * keeps[k]
        return hr, hi, er, ei, qr, qi, kr

    br, bi = chain(nil, nil, 1, None)
    kb = one[:, :LANE]
    for g in range(SEGS):
        kb = kb * seg[2, g:g + 1, 0:LANE]
    msg_fz[z, :, 0:states] = br
    msg_fz[z, :, states:2 * states] = bi
    msg_fz[z, :, 2 * states:] = kb
    spread(msg_fz, fz_s, fz_r, z, z_peers, at_z)

    advance(2)
    load_w.wait()
    depth = w_wide.shape[1]

    def part_weights(n, carry):
        at = pl.ds(pl.multiple_of(n * depth, depth), depth)
        block = w_raw[at].astype(F32)
        w_wide[0] = block[:, 0, :]
        w_wide[1] = block[:, 1, :]
        w_ref[0, at, :] = w_wide[0].astype(BF16)
        w_ref[1, at, :] = w_wide[1].astype(BF16)
        return carry

    parts = slab // depth
    lax.fori_loop(0, parts, part_weights, 0)

    for p in y_peers:
        arrived(cslab.at[p], slab_r.at[p])
        for h in range(2):
            ps_send[p, h] = jnp.dot(cslab[p], w_ref[h], preferred_element_type=F32).astype(BF16)
            copy(ps_send.at[p, h], ps_recv.at[y, h], ps_s, ps_r, at_y(p)).start()
    departed(ps_send.at[pl.ds(0, ny - 1)], ps_s)
    advance(2)

    collect(msg_fz, fz_r, z_peers)
    keeps_z = [msg_fz[k, :, 2 * states:] for k in range(nz)]
    hr, hi, er, ei, qr, qi, kx = across(msg_fz, z, nz, blk_r, blk_i, 1, keeps_z)
    msg_fx[x, :, 0:states] = hr
    msg_fx[x, :, states:2 * states] = hi
    msg_fx[x, :, 2 * states:] = kx
    spread(msg_fx, fx_s, fx_r, x, x_peers, at_x)

    advance(2)
    own = cga[z, y]
    for h, ref in ((0, sg_r), (1, sg_i)):
        share = jnp.dot(own, w_ref[h], preferred_element_type=F32)
        for j in range(tiles):
            ref[j] = share[:, lanes_of(j)]
    collect(msg_fx, fx_r, x_peers)
    keeps_x = [msg_fx[k, :, 2 * states:] for k in range(nx)]
    _, _, fr, fi, _, _, _ = across(msg_fx, x, nx, row_r, row_i, 1, keeps_x)
    mr, mi = cmul(qr, qi, fr, fi)
    chain(mr + er, mi + ei, 1, carry_f)

    def fill(i, held):
        sr, si = held
        kk = wide(keep_at(i), states)
        tr, ti = cmul(lr, li, sr, si)
        sr = kk * tr + gain * rows(ur, i)
        si = kk * ti + gain * rows(ui, i)
        put_rows(st_r, i, sr)
        put_rows(st_i, i, si)
        return sr, si

    lax.fori_loop(0, steps, fill, (carry_f[0], carry_f[1]))
    for k in range(nz):
        half[k, :, 0:LANE] = st_r[k].astype(BF16)
        half[k, :, LANE:] = st_i[k].astype(BF16)
    for p in z_peers:
        copy(half.at[p], sga.at[z], sg_s, sg_rs, at_z(p)).start()
    departed(half.at[pl.ds(0, nz - 1)], sg_s)
    sga[z] = half[z]
    advance(2)


    def project(stage):
        count = nz * tokens
        if stage == 0:
            state_t[...] = sga[...].reshape(count, 2 * LANE).T
        for q in range(stage * nc, (stage + 1) * nc):
            block = cga[:, q].reshape(count, slab)
            grad = jnp.dot(state_t[...], block, preferred_element_type=F32)
            for k in range(nx):
                grads[q, k] = grad[:, lanes_of(k)]
                out_x[k, q] = grad[:, lanes_of(k)].astype(BF16)
            for p in x_peers:
                copy(out_x.at[p, q], recv_x.at[x, q], x_s, x_r, at_x(p)).start()

    ring_end(0)
    collect(sga, sg_rs, z_peers)
    project(0)
    advance(len(todo))

    arrived(ps_recv.at[pl.ds(0, ny - 1)], ps_r)
    for p in y_peers:
        for h, ref in ((0, sg_r), (1, sg_i)):
            for j in range(tiles):
                ref[j] += ps_recv[p, h, :, lanes_of(j)].astype(F32)

    def some(ref, i, group):
        at = pl.ds(i, SEGS, stride=steps)
        return jnp.concatenate([ref[j, at, :] for j in group], axis=1)

    def back_step(group, i, held, prior_r, prior_i):
        hr, hi, tr, ti, wr, wi, qr, qi, wg, rr, ri = held
        cols = slice(group[0] * LANE, (group[-1] + 1) * LANE)
        kk = wide(keep_at(i), len(group) * LANE)
        vr, vi = some(ur, i, group), some(ui, i, group)
        xr, xi = some(sg_r, i, group) + hr, some(sg_i, i, group) + hi
        pr, pi = kk * prior_r, kk * prior_i
        wr, wi = wr + (xr * pr + xi * pi), wi + (xi * pr - xr * pi)
        qr, qi = qr + (tr * pr + ti * pi), qi + (ti * pr - tr * pi)
        wg = wg + (xr * vr + xi * vi)
        rr, ri = rr + (tr * vr + ti * vi), ri + (ti * vr - tr * vi)
        ar, ai = kk * lr[:, cols], kk * -li[:, cols]
        hr, hi = cmul(ar, ai, xr, xi)
        tr, ti = cmul(ar, ai, tr, ti)
        return hr, hi, tr, ti, wr, wi, qr, qi, wg, rr, ri

    span = max(1, tiles // 4)
    for first in range(0, tiles, span):
        group = range(first, first + span)
        cols = slice(first * LANE, (first + span) * LANE)
        none = jnp.zeros((SEGS, span * LANE), F32)
        held = (none, none, none + 1.0) + (none,) * 8

        def back(n, held, group=group):
            i = steps - 1 - n
            return back_step(group, i, held, some(st_r, i - 1, group), some(st_i, i - 1, group))

        held = lax.fori_loop(0, steps - 1, back, held)
        held = back_step(group, 0, held, carry_f[0, :, cols], carry_f[1, :, cols])
        for k, value in enumerate(held):
            bseg[k, :, cols] = value

    def fold(held, parts, link):
        hr, hi, pr, pi, wr, wi, qr, qi, wg, rr, ri = held
        br, bi, vr, vi, sr, si, sg, ur_, ui_ = parts
        mr, mi = cmul(sr, si, hr, hi)
        wr, wi = wr + (vr + mr), wi + (vi + mi)
        mr, mi = cmul(sr, si, pr, pi)
        qr, qi = qr + mr, qi + mi
        wg = wg + (sg + (ur_ * hr - ui_ * hi))
        mr, mi = cmul(ur_, ui_, pr, pi)
        rr, ri = rr + mr, ri + mi
        mr, mi = cmul(*link, hr, hi)
        hr, hi = mr + br, mi + bi
        pr, pi = cmul(*link, pr, pi)
        return hr, hi, pr, pi, wr, wi, qr, qi, wg, rr, ri

    fresh = (nil, nil, one) + (nil,) * 8

    def row_of(k, g):
        return bseg[k, g:g + 1]

    held = fresh
    for g in range(SEGS - 1, -1, -1):
        for k in range(4):
            carry_b[k, g:g + 1] = held[k]
        parts = [row_of(k, g) for k in (0, 1, 4, 5, 6, 7, 8, 9, 10)]
        held = fold(held, parts, (row_of(2, g), row_of(3, g)))

    def put(buf, mine, values):
        for k, value in enumerate(values):
            buf[mine, :, k * states:(k + 1) * states] = value

    def join(buf, mine, n, ar, ai, keeps):
        held = fresh
        mark = fresh[:4]
        for k in range(n - 1, -1, -1):
            here = k == mine
            mark = [jnp.where(here, new, old) for new, old in zip(held[:4], mark)]
            kw = wide(keeps[k], states)
            parts = [buf[k, :, m * states:(m + 1) * states] for m in range(9)]
            held = fold(held, parts, (kw * ar, kw * -ai))
        return held, mark

    put(msg_bz, z, held[:2] + held[4:])
    spread(msg_bz, bz_s, bz_r, z, z_peers, at_z)
    for stage in range(1, stages):
        ring_end(stage)
        project(stage)
    collect(msg_bz, bz_r, z_peers)
    held, (er, ei, qr, qi) = join(msg_bz, z, nz, blk_r, blk_i, keeps_z)
    put(msg_bx, x, held[:2] + held[4:])
    spread(msg_bx, bx_s, bx_r, x, x_peers, at_x)
    if nx > 1:
        arrived(recv_x.at[pl.ds(0, nx - 1)], x_r)
        departed(out_x.at[pl.ds(0, nx - 1)], x_s)
    for q in range(ny):
        grad = grads[q, x]
        for p in x_peers:
            grad = grad + recv_x[p, q].astype(F32)
        grads[q, 0] = grad
        out_y[q] = grad.astype(BF16)
    for p in y_peers:
        copy(out_y.at[p], recv_y.at[y], y_s, y_r, at_y(p)).start()
    settle()
    collect(msg_bx, bx_r, x_peers)
    held, (fr, fi, _, _) = join(msg_bx, x, nx, row_r, row_i, keeps_x)
    put(msg_sy, y, (held[4], held[5], held[8]))
    spread(msg_sy, sy_s, sy_r, y, y_peers, at_y)
    if ny > 1:
        arrived(recv_y.at[pl.ds(0, ny - 1)], y_r)
        departed(out_y.at[pl.ds(0, ny - 1)], y_s)
    grad = grads[y, 0]
    for p in y_peers:
        grad = grad + recv_y[p].astype(F32)
    out_z[...] = grad.T.reshape(out_z.shape)
    for p in z_peers:
        copy(out_z.at[p], recv_z.at[z], z_s, z_r, at_z(p)).start()
    departed(out_z.at[pl.ds(0, nz - 1)], z_s)
    recv_z[z] = out_z[z]

    mr, mi = cmul(qr, qi, fr, fi)
    mr, mi = cmul(carry_b[2], carry_b[3], mr + er, mi + ei)

    def adjoint(n, held):
        i = steps - 1 - n
        hr, hi = held
        kk = wide(keep_at(i), states)
        ar = rows(sg_r, i) + hr
        ai = rows(sg_i, i) + hi
        put_rows(sg_r, i, gain * ar)
        put_rows(sg_i, i, gain * ai)
        tr, ti = cmul(lr, -li, ar, ai)
        return kk * tr, kk * ti

    lax.fori_loop(0, steps, adjoint, (carry_b[0] + mr, carry_b[1] + mi))
    for h, ref in ((0, sg_r), (1, sg_i)):
        gin_raw[:, h, :] = jnp.concatenate([ref[j].astype(BF16) for j in range(tiles)], axis=1)
    store_gin = pltpu.make_async_copy(gin_raw, gin_ref, load_s.at[0])
    store_gin.start()


    collect(msg_sy, sy_r, y_peers)
    sums = msg_sy[0]
    for k in range(1, ny):
        sums = sums + msg_sy[k]
    geig_ref[0:1] = sums[:, 0:states]
    geig_ref[1:2] = sums[:, states:2 * states]
    ggain_ref[...] = sums[:, 2 * states:]

    collect(recv_z, z_r, z_peers)
    for k in range(nz):
        for h in range(2):
            gproj_ref[:, h, lanes_of(k)] = recv_z[k, :, lanes_of(h)]

    settle()
    store_gin.wait()


def hand_over(*refs):
    count = len(refs) // 2
    for k in range(count):
        refs[count + k][...] = refs[k][...]


def body(dims, inputs, cotangent, out_proj, modulus, phase, gain, retain, doc_starts, row_blocks):
    ny, nx, nz, nc = dims
    _, tokens, _, states = inputs.shape
    width = cotangent.shape[2]
    slab = width // ny
    stages = ny // nc
    rows_z = LANE // nz
    dma = pltpu.SemaphoreType.DMA

    line = 2 * states + LANE
    scratch = [
        pltpu.VMEM((tokens, 2, states), BF16),
        pltpu.VMEM((tokens, 2, states), BF16),
        pltpu.VMEM((tokens, width), BF16),
        pltpu.VMEM((slab, 2, states), BF16),
        pltpu.VMEM((2, LANE, states), F32),
        pltpu.VMEM((2, slab, states), BF16),
        pltpu.VMEM((tokens, LANE), F32),
        *[pltpu.VMEM((states // LANE, tokens, LANE), F32) for _ in range(6)],
        pltpu.VMEM((3, SEGS, states), F32),
        pltpu.VMEM((11, SEGS, states), F32),
        pltpu.VMEM((2, SEGS, states), F32), pltpu.VMEM((4, SEGS, states), F32),
        pltpu.VMEM((nz, ny, tokens, slab), BF16),
        pltpu.VMEM((ny, tokens, slab), BF16),
        pltpu.VMEM((ny, 2, tokens, states), BF16), pltpu.VMEM((ny, 2, tokens, states), BF16),
        pltpu.VMEM((nz, tokens, 2 * LANE), BF16), pltpu.VMEM((nz, tokens, 2 * LANE), BF16),
        pltpu.VMEM((2 * LANE, nz * tokens), BF16),
        pltpu.VMEM((ny, nx, 2 * LANE, LANE), F32),
        pltpu.VMEM((nx, ny, 2 * LANE, LANE), BF16), pltpu.VMEM((nx, ny, 2 * LANE, LANE), BF16),
        pltpu.VMEM((ny, 2 * LANE, LANE), BF16), pltpu.VMEM((ny, 2 * LANE, LANE), BF16),
        pltpu.VMEM((nz, rows_z, 2 * LANE), F32), pltpu.VMEM((nz, rows_z, 2 * LANE), F32),
        pltpu.VMEM((nz, 1, line), F32), pltpu.VMEM((nx, 1, line), F32),
        pltpu.VMEM((nz, 1, 9 * states), F32), pltpu.VMEM((nx, 1, 9 * states), F32),
        pltpu.VMEM((ny, 1, 3 * states), F32),
        dma((3,)), dma, dma((ny,)), dma((stages,)), dma((stages, 2, nz)), dma((stages,)), dma((stages,)),
        *[dma for _ in range(10)],
        *[dma for _ in range(10)],
    ]
    vmem = pl.BlockSpec(memory_space=pltpu.VMEM)
    smem = pl.BlockSpec(memory_space=pltpu.SMEM)
    hbm = pl.BlockSpec(memory_space=pl.ANY)
    results = pl.pallas_call(
        functools.partial(kernel, dims),
        out_shape=(
            jax.ShapeDtypeStruct((tokens, 2, states), BF16),
            jax.ShapeDtypeStruct((rows_z, 2, states), F32),
            jax.ShapeDtypeStruct((2, states), F32),
            jax.ShapeDtypeStruct((1, states), F32),
        ),
        in_specs=[smem, vmem, vmem, vmem, vmem, vmem, hbm, hbm, hbm],
        out_specs=(hbm, vmem, vmem, vmem),
        scratch_shapes=scratch,
        compiler_params=pltpu.CompilerParams(
            collective_id=0, has_side_effects=True, vmem_limit_bytes=56 * 1024 * 1024
        ),
    )(
        doc_starts, row_blocks[None], modulus[None], phase[None], gain[None], retain,
        inputs[0], cotangent[0], out_proj,
    )
    grad_inputs, grad_proj, grad_eigen, grad_gain = pl.pallas_call(
        hand_over,
        out_shape=tuple(jax.ShapeDtypeStruct(r.shape, r.dtype) for r in results),
        in_specs=[vmem] * 4,
        out_specs=(vmem,) * 4,
    )(*results)
    return grad_inputs[None], grad_proj, grad_eigen, grad_gain[0]


def solution(mesh):
    sizes = mesh.shape
    nx, nz = grid_of(sizes["ctx"])
    dims = (sizes["dp"], nx, nz, sizes["chan"])
    return jax.shard_map(
        functools.partial(body, dims),
        mesh=mesh,
        in_specs=(
            P("dp", "ctx", None, "chan"),
            P("dp", "ctx", None),
            P("dp", None, "chan"),
            P("chan"),
            P("chan"),
            P("chan"),
            P("dp", "ctx"),
            P("dp", None),
            P("dp"),
        ),
        out_specs=(
            P("dp", "ctx", None, "chan"),
            P(("dp", "ctx"), None, "chan"),
            P(None, "chan"),
            P("chan"),
        ),
        check_vma=False,
    )
```

```python
import functools

import jax
import jax.numpy as jnp
from jax import lax
from jax.experimental import pallas as pl
from jax.experimental.pallas import tpu as pltpu
from jax.sharding import PartitionSpec as P

MESH = pl.DeviceIdType.MESH
F32 = jnp.float32
BF16 = jnp.bfloat16
LANE = 128
SEGS = 8


def grid_of(ctx):
    z = {32: 8, 4: 2, 8: 4}[ctx]
    return ctx // z, z


def cmul(ar, ai, br, bi):
    return ar * br - ai * bi, ar * bi + ai * br


def wide(row, states):
    return jnp.concatenate([row] * (states // LANE), axis=1)


def lanes_of(j):
    return slice(j * LANE, (j + 1) * LANE)


def nearest_last(n):
    return sorted(range(1, n), key=lambda k: -min(k, n - k))


def kernel(
    dims,
    starts_ref, blocks_ref, mod_ref, phase_ref, gain_ref, retain_ref, u_hbm, cot_hbm, w_hbm,
    gin_ref, gproj_ref, geig_ref, ggain_ref,
    gin_raw, u_raw, cot_raw, w_raw, w_wide, w_ref, mask,
    ur, ui, st_r, st_i, sg_r, sg_i, seg, bseg, carry_f, carry_b,
    cga, cslab, ps_send, ps_recv, half, sga, state_t, grads, out_x, recv_x, out_y, recv_y, out_z, recv_z,
    msg_fz, msg_fx, msg_bz, msg_bx, msg_sy,
    load_s, slab_s, slab_r, ag_s, ag_r, dd_s, dd_r, ps_s, ps_r, sg_s, sg_rs,
    x_s, x_r, y_s, y_r, z_s, z_r,
    fz_s, fz_r, fx_s, fx_r, bz_s, bz_r, bx_s, bx_r, sy_s, sy_r,
):
    ny, nx, nz, nc = dims
    tokens, width = cot_raw.shape
    tiles = ur.shape[0]
    states = tiles * LANE
    steps = tokens // SEGS
    slab = width // ny
    stages = ny // nc
    y = lax.axis_index("dp")
    ctx = lax.axis_index("ctx")
    c = lax.axis_index("chan")
    x, z = ctx // nz, ctx % nz

    def at_z(other):
        return (y, x * nz + other, c)

    def at_x(other):
        return (y, other * nz + z, c)

    def at_y(other):
        return (other, ctx, c)

    sibling = (y, ctx, 1 - c)
    z_peers = [(z + k) % nz for k in nearest_last(nz)]
    x_peers = [(x + k) % nx for k in nearest_last(nx)]
    y_peers = [(y + k) % ny for k in nearest_last(ny)]

    def copy(src, dst, ssem, rsem, device):
        return pltpu.make_async_remote_copy(
            src_ref=src, dst_ref=dst, send_sem=ssem, recv_sem=rsem,
            device_id=device, device_id_type=MESH,
        )

    barrier = pltpu.get_barrier_semaphore()
    greeted = [at_z(p) for p in z_peers] + [at_x(p) for p in x_peers]
    greeted += [at_y(p) for p in y_peers] + [sibling]
    for device in greeted:
        pl.semaphore_signal(barrier, inc=1, device_id=device, device_id_type=MESH)
    load_cot = pltpu.make_async_copy(cot_hbm, cot_raw, load_s.at[0])
    load_u = pltpu.make_async_copy(u_hbm, u_raw, load_s.at[1])
    load_w = pltpu.make_async_copy(w_hbm, w_raw, load_s.at[2])
    load_cot.start()
    load_u.start()
    load_w.start()

    alive = jnp.where(ctx < blocks_ref[...], 1.0, 0.0)
    alive = jnp.broadcast_to(alive, (tokens, slab)).astype(BF16)
    load_cot.wait()
    for q in range(ny):
        cga[z, q] = cot_raw[:, q * slab:(q + 1) * slab] * alive
    pl.semaphore_wait(barrier, len(greeted))

    def arrived(view, rsem):
        copy(view, view, rsem, rsem, sibling).wait_recv()

    def departed(view, ssem):
        pending.append(copy(view, view, ssem, ssem, sibling))

    def settle():
        for s in pending:
            s.wait_send()
        pending.clear()

    def spread(buf, ssem, rsem, mine, peers, where):
        for p in peers:
            copy(buf.at[mine], buf.at[mine], ssem, rsem, where(p)).start()
        if peers:
            departed(buf.at[pl.ds(0, len(peers))], ssem)

    def collect(buf, rsem, peers):
        if peers:
            arrived(buf.at[pl.ds(0, len(peers))], rsem)

    pending = []

    for p in y_peers:
        copy(cga.at[z, p], cslab.at[y], slab_s, slab_r.at[y], at_y(p)).start()
    departed(cslab.at[pl.ds(0, ny - 1)], slab_s)

    hops = nz // 2
    split = tokens // 2

    def ring_part(slot, q, k, way):
        if k < hops or nz % 2:
            return cga.at[slot, q]
        return cga.at[slot, q, pl.ds(way * split, split)]

    def ring_step(stage, k):
        q = stage * nc + c
        for way in range(2):
            sign = -1 if way == 0 else 1
            slot = (z + sign * k) % nz
            if k >= 1:
                arrived(ring_part(slot, q, k, way), ag_r.at[stage, way, k])
            if k < hops:
                part = ring_part(slot, q, k + 1, way)
                to = at_z((z - sign) % nz)
                copy(part, part, ag_s.at[stage], ag_r.at[stage, way, k + 1], to).start()
            if k >= 1:
                part = ring_part(slot, q, k, way)
                copy(part, part, dd_s.at[stage], dd_r.at[stage], sibling).start()
        if k == hops:
            departed(cga.at[pl.ds(0, nz - 1), q], ag_s.at[stage])
            departed(cga.at[pl.ds(0, nz - 1), q], dd_s.at[stage])

    def ring_end(stage):
        arrived(cga.at[pl.ds(0, nz - 1), stage * nc + 1 - c], dd_r.at[stage])

    todo = sorted(
        [(stage, k) for k in range(hops + 1) for stage in range(stages)],
        key=lambda step: (step[0] + step[1], step[0]),
    )

    def advance(count=1):
        for _ in range(min(count, len(todo))):
            ring_step(*todo.pop(0))

    advance()

    row = lax.broadcasted_iota(jnp.int32, (1, tokens), 1) + ctx * tokens
    keep = retain_ref[...]
    for k in range(starts_ref.shape[1]):
        keep = jnp.where(row == starts_ref[0, k], 0.0, keep)
    mask[...] = jnp.broadcast_to(keep, (LANE, tokens)).T

    lr1 = mod_ref[...] * jnp.cos(phase_ref[...])
    li1 = mod_ref[...] * jnp.sin(phase_ref[...])
    shape = (SEGS, states)
    lr = jnp.broadcast_to(lr1, shape)
    li = jnp.broadcast_to(li1, shape)
    gain = jnp.broadcast_to(gain_ref[...], shape)

    def power(br, bi, n):
        while n > 1:
            br, bi = cmul(br, bi, br, bi)
            n //= 2
        return br, bi

    seg_r, seg_i = power(lr1, li1, steps)
    blk_r, blk_i = power(seg_r, seg_i, SEGS)
    row_r, row_i = power(blk_r, blk_i, nz)

    load_u.wait()
    drive = u_raw[...].astype(F32)
    for j in range(tiles):
        ur[j] = drive[:, 0, lanes_of(j)]
        ui[j] = drive[:, 1, lanes_of(j)]

    def rows(ref, i):
        at = pl.ds(i, SEGS, stride=steps)
        return jnp.concatenate([ref[j, at, :] for j in range(tiles)], axis=1)

    def put_rows(ref, i, value):
        for j in range(tiles):
            ref[j, pl.ds(i, SEGS, stride=steps), :] = value[:, lanes_of(j)]

    def keep_at(i):
        return mask[pl.ds(i, SEGS, stride=steps), :]

    def summary(i, held):
        sr, si, kp = held
        k = keep_at(i)
        kk = wide(k, states)
        tr, ti = cmul(lr, li, sr, si)
        return kk * tr + gain * rows(ur, i), kk * ti + gain * rows(ui, i), kp * k

    zero = jnp.zeros(shape, F32)
    sr, si, kp = lax.fori_loop(0, steps, summary, (zero, zero, jnp.ones((SEGS, LANE), F32)))
    seg[0] = sr
    seg[1] = si
    seg[2] = wide(kp, states)

    def chain(hr, hi, sign, hold):
        order = range(SEGS) if sign > 0 else range(SEGS - 1, -1, -1)
        for g in order:
            if hold is not None:
                hold[0, g:g + 1] = hr
                hold[1, g:g + 1] = hi
            pr, pi = cmul(seg_r, sign * seg_i, hr, hi)
            kg = seg[2, g:g + 1]
            hr = kg * pr + seg[0, g:g + 1]
            hi = kg * pi + seg[1, g:g + 1]
        return hr, hi

    one = jnp.ones((1, states), F32)
    nil = jnp.zeros((1, states), F32)

    def across(buf, mine, n, ar, ai, sign, keeps):
        order = range(n) if sign > 0 else range(n - 1, -1, -1)
        hr, hi, pr, pi, kr = nil, nil, one, nil, one[:, :LANE]
        er, ei, qr, qi = nil, nil, one, nil
        for k in order:
            here = k == mine
            er = jnp.where(here, hr, er)
            ei = jnp.where(here, hi, ei)
            qr = jnp.where(here, pr, qr)
            qi = jnp.where(here, pi, qi)
            kw = wide(keeps[k], states)
            mr, mi = cmul(ar, sign * ai, hr, hi)
            hr = kw * mr + buf[k, :, 0:states]
            hi = kw * mi + buf[k, :, states:2 * states]
            mr, mi = cmul(ar, sign * ai, pr, pi)
            pr, pi = kw * mr, kw * mi
            kr = kr * keeps[k]
        return hr, hi, er, ei, qr, qi, kr

    br, bi = chain(nil, nil, 1, None)
    kb = one[:, :LANE]
    for g in range(SEGS):
        kb = kb * seg[2, g:g + 1, 0:LANE]
    msg_fz[z, :, 0:states] = br
    msg_fz[z, :, states:2 * states] = bi
    msg_fz[z, :, 2 * states:] = kb
    spread(msg_fz, fz_s, fz_r, z, z_peers, at_z)

    advance(2)
    load_w.wait()
    depth = w_wide.shape[1]

    def part_weights(n, carry):
        at = pl.ds(pl.multiple_of(n * depth, depth), depth)
        block = w_raw[at].astype(F32)
        w_wide[0] = block[:, 0, :]
        w_wide[1] = block[:, 1, :]
        w_ref[0, at, :] = w_wide[0].astype(BF16)
        w_ref[1, at, :] = w_wide[1].astype(BF16)
        return carry

    parts = slab // depth
    lax.fori_loop(0, parts, part_weights, 0)

    for p in y_peers:
        arrived(cslab.at[p], slab_r.at[p])
        for h in range(2):
            ps_send[p, h] = jnp.dot(cslab[p], w_ref[h], preferred_element_type=F32).astype(BF16)
            copy(ps_send.at[p, h], ps_recv.at[y, h], ps_s, ps_r, at_y(p)).start()
    departed(ps_send.at[pl.ds(0, ny - 1)], ps_s)
    advance(2)

    collect(msg_fz, fz_r, z_peers)
    keeps_z = [msg_fz[k, :, 2 * states:] for k in range(nz)]
    hr, hi, er, ei, qr, qi, kx = across(msg_fz, z, nz, blk_r, blk_i, 1, keeps_z)
    msg_fx[x, :, 0:states] = hr
    msg_fx[x, :, states:2 * states] = hi
    msg_fx[x, :, 2 * states:] = kx
    spread(msg_fx, fx_s, fx_r, x, x_peers, at_x)

    advance(2)
    own = cga[z, y]
    for h, ref in ((0, sg_r), (1, sg_i)):
        share = jnp.dot(own, w_ref[h], preferred_element_type=F32)
        for j in range(tiles):
            ref[j] = share[:, lanes_of(j)]
    collect(msg_fx, fx_r, x_peers)
    keeps_x = [msg_fx[k, :, 2 * states:] for k in range(nx)]
    _, _, fr, fi, _, _, _ = across(msg_fx, x, nx, row_r, row_i, 1, keeps_x)
    mr, mi = cmul(qr, qi, fr, fi)
    chain(mr + er, mi + ei, 1, carry_f)

    def fill(i, held):
        sr, si = held
        kk = wide(keep_at(i), states)
        tr, ti = cmul(lr, li, sr, si)
        sr = kk * tr + gain * rows(ur, i)
        si = kk * ti + gain * rows(ui, i)
        put_rows(st_r, i, sr)
        put_rows(st_i, i, si)
        return sr, si

    lax.fori_loop(0, steps, fill, (carry_f[0], carry_f[1]))
    for k in range(nz):
        half[k, :, 0:LANE] = st_r[k].astype(BF16)
        half[k, :, LANE:] = st_i[k].astype(BF16)
    for p in z_peers:
        copy(half.at[p], sga.at[z], sg_s, sg_rs, at_z(p)).start()
    departed(half.at[pl.ds(0, nz - 1)], sg_s)
    sga[z] = half[z]
    advance(2)


    def some(ref, i, group):
        at = pl.ds(i, SEGS, stride=steps)
        return jnp.concatenate([ref[j, at, :] for j in group], axis=1)

    span = max(1, tiles // 4)

    def sweep(step, count, ones, places):
        for first in range(0, tiles, span):
            group = range(first, first + span)
            cols = slice(first * LANE, (first + span) * LANE)
            none = jnp.zeros((SEGS, span * LANE), F32)
            held = (none + 1.0,) * ones + (none,) * (count - ones)

            def back(n, held, group=group):
                i = steps - 1 - n
                return step(group, i, held, some(st_r, i - 1, group), some(st_i, i - 1, group))

            held = lax.fori_loop(0, steps - 1, back, held)
            held = step(group, 0, held, carry_f[0, :, cols], carry_f[1, :, cols])
            for k, value in zip(places, held):
                bseg[k, :, cols] = value

    def reach_step(group, i, held, prior_r, prior_i):
        tr, ti, qr, qi, rr, ri = held
        cols = slice(group[0] * LANE, (group[-1] + 1) * LANE)
        kk = wide(keep_at(i), len(group) * LANE)
        vr, vi = some(ur, i, group), some(ui, i, group)
        pr, pi = kk * prior_r, kk * prior_i
        qr, qi = qr + (tr * pr + ti * pi), qi + (ti * pr - tr * pi)
        rr, ri = rr + (tr * vr + ti * vi), ri + (ti * vr - tr * vi)
        tr, ti = cmul(kk * lr[:, cols], kk * -li[:, cols], tr, ti)
        return tr, ti, qr, qi, rr, ri

    sweep(reach_step, 6, 1, (2, 3, 6, 7, 9, 10))

    def project(stage):
        count = nz * tokens
        if stage == 0:
            state_t[...] = sga[...].reshape(count, 2 * LANE).T
        for q in range(stage * nc, (stage + 1) * nc):
            block = cga[:, q].reshape(count, slab)
            grad = jnp.dot(state_t[...], block, preferred_element_type=F32)
            for k in range(nx):
                grads[q, k] = grad[:, lanes_of(k)]
                out_x[k, q] = grad[:, lanes_of(k)].astype(BF16)
            for p in x_peers:
                copy(out_x.at[p, q], recv_x.at[x, q], x_s, x_r, at_x(p)).start()

    ring_end(0)
    collect(sga, sg_rs, z_peers)
    project(0)
    advance(len(todo))

    arrived(ps_recv.at[pl.ds(0, ny - 1)], ps_r)
    for h, ref in ((0, sg_r), (1, sg_i)):
        for j in range(tiles):
            share = ref[j]
            for p in y_peers:
                share = share + ps_recv[p, h, :, lanes_of(j)].astype(F32)
            ref[j] = share

    def back_step(group, i, held, prior_r, prior_i):
        hr, hi, wr, wi, wg = held
        cols = slice(group[0] * LANE, (group[-1] + 1) * LANE)
        kk = wide(keep_at(i), len(group) * LANE)
        xr, xi = some(sg_r, i, group) + hr, some(sg_i, i, group) + hi
        pr, pi = kk * prior_r, kk * prior_i
        wr, wi = wr + (xr * pr + xi * pi), wi + (xi * pr - xr * pi)
        wg = wg + (xr * some(ur, i, group) + xi * some(ui, i, group))
        hr, hi = cmul(kk * lr[:, cols], kk * -li[:, cols], xr, xi)
        return hr, hi, wr, wi, wg

    sweep(back_step, 5, 0, (0, 1, 4, 5, 8))

    def fold(held, parts, link):
        hr, hi, pr, pi, wr, wi, qr, qi, wg, rr, ri = held
        br, bi, vr, vi, sr, si, sg, ur_, ui_ = parts
        mr, mi = cmul(sr, si, hr, hi)
        wr, wi = wr + (vr + mr), wi + (vi + mi)
        mr, mi = cmul(sr, si, pr, pi)
        qr, qi = qr + mr, qi + mi
        wg = wg + (sg + (ur_ * hr - ui_ * hi))
        mr, mi = cmul(ur_, ui_, pr, pi)
        rr, ri = rr + mr, ri + mi
        mr, mi = cmul(*link, hr, hi)
        hr, hi = mr + br, mi + bi
        pr, pi = cmul(*link, pr, pi)
        return hr, hi, pr, pi, wr, wi, qr, qi, wg, rr, ri

    fresh = (nil, nil, one) + (nil,) * 8

    def row_of(k, g):
        return bseg[k, g:g + 1]

    held = fresh
    for g in range(SEGS - 1, -1, -1):
        for k in range(4):
            carry_b[k, g:g + 1] = held[k]
        parts = [row_of(k, g) for k in (0, 1, 4, 5, 6, 7, 8, 9, 10)]
        held = fold(held, parts, (row_of(2, g), row_of(3, g)))

    def put(buf, mine, values):
        for k, value in enumerate(values):
            buf[mine, :, k * states:(k + 1) * states] = value

    def join(buf, mine, n, ar, ai, keeps):
        held = fresh
        mark = fresh[:4]
        for k in range(n - 1, -1, -1):
            here = k == mine
            mark = [jnp.where(here, new, old) for new, old in zip(held[:4], mark)]
            kw = wide(keeps[k], states)
            parts = [buf[k, :, m * states:(m + 1) * states] for m in range(9)]
            held = fold(held, parts, (kw * ar, kw * -ai))
        return held, mark

    put(msg_bz, z, held[:2] + held[4:])
    spread(msg_bz, bz_s, bz_r, z, z_peers, at_z)
    for stage in range(1, stages):
        ring_end(stage)
        project(stage)
    collect(msg_bz, bz_r, z_peers)
    held, (er, ei, qr, qi) = join(msg_bz, z, nz, blk_r, blk_i, keeps_z)
    put(msg_bx, x, held[:2] + held[4:])
    spread(msg_bx, bx_s, bx_r, x, x_peers, at_x)
    if nx > 1:
        arrived(recv_x.at[pl.ds(0, nx - 1)], x_r)
        departed(out_x.at[pl.ds(0, nx - 1)], x_s)
    for q in range(ny):
        grad = grads[q, x]
        for p in x_peers:
            grad = grad + recv_x[p, q].astype(F32)
        grads[q, 0] = grad
        out_y[q] = grad.astype(BF16)
    for p in y_peers:
        copy(out_y.at[p], recv_y.at[y], y_s, y_r, at_y(p)).start()
    settle()
    collect(msg_bx, bx_r, x_peers)
    held, (fr, fi, _, _) = join(msg_bx, x, nx, row_r, row_i, keeps_x)
    put(msg_sy, y, (held[4], held[5], held[8]))
    spread(msg_sy, sy_s, sy_r, y, y_peers, at_y)
    if ny > 1:
        arrived(recv_y.at[pl.ds(0, ny - 1)], y_r)
        departed(out_y.at[pl.ds(0, ny - 1)], y_s)
    grad = grads[y, 0]
    for p in y_peers:
        grad = grad + recv_y[p].astype(F32)
    out_z[...] = grad.T.reshape(out_z.shape)
    for p in z_peers:
        copy(out_z.at[p], recv_z.at[z], z_s, z_r, at_z(p)).start()
    departed(out_z.at[pl.ds(0, nz - 1)], z_s)
    recv_z[z] = out_z[z]

    mr, mi = cmul(qr, qi, fr, fi)
    mr, mi = cmul(carry_b[2], carry_b[3], mr + er, mi + ei)

    def adjoint(n, held):
        i = steps - 1 - n
        hr, hi = held
        kk = wide(keep_at(i), states)
        ar = rows(sg_r, i) + hr
        ai = rows(sg_i, i) + hi
        put_rows(sg_r, i, gain * ar)
        put_rows(sg_i, i, gain * ai)
        tr, ti = cmul(lr, -li, ar, ai)
        return kk * tr, kk * ti

    lax.fori_loop(0, steps, adjoint, (carry_b[0] + mr, carry_b[1] + mi))
    for h, ref in ((0, sg_r), (1, sg_i)):
        gin_raw[:, h, :] = jnp.concatenate([ref[j].astype(BF16) for j in range(tiles)], axis=1)
    store_gin = pltpu.make_async_copy(gin_raw, gin_ref, load_s.at[0])
    store_gin.start()


    collect(msg_sy, sy_r, y_peers)
    sums = msg_sy[0]
    for k in range(1, ny):
        sums = sums + msg_sy[k]
    geig_ref[0:1] = sums[:, 0:states]
    geig_ref[1:2] = sums[:, states:2 * states]
    ggain_ref[...] = sums[:, 2 * states:]

    collect(recv_z, z_r, z_peers)
    for k in range(nz):
        for h in range(2):
            gproj_ref[:, h, lanes_of(k)] = recv_z[k, :, lanes_of(h)]

    settle()
    store_gin.wait()


def hand_over(*refs):
    count = len(refs) // 2
    for k in range(count):
        refs[count + k][...] = refs[k][...]


def body(dims, inputs, cotangent, out_proj, modulus, phase, gain, retain, doc_starts, row_blocks):
    ny, nx, nz, nc = dims
    _, tokens, _, states = inputs.shape
    width = cotangent.shape[2]
    slab = width // ny
    stages = ny // nc
    rows_z = LANE // nz
    dma = pltpu.SemaphoreType.DMA

    line = 2 * states + LANE
    scratch = [
        pltpu.VMEM((tokens, 2, states), BF16),
        pltpu.VMEM((tokens, 2, states), BF16),
        pltpu.VMEM((tokens, width), BF16),
        pltpu.VMEM((slab, 2, states), BF16),
        pltpu.VMEM((2, LANE, states), F32),
        pltpu.VMEM((2, slab, states), BF16),
        pltpu.VMEM((tokens, LANE), F32),
        *[pltpu.VMEM((states // LANE, tokens, LANE), F32) for _ in range(6)],
        pltpu.VMEM((3, SEGS, states), F32),
        pltpu.VMEM((11, SEGS, states), F32),
        pltpu.VMEM((2, SEGS, states), F32), pltpu.VMEM((4, SEGS, states), F32),
        pltpu.VMEM((nz, ny, tokens, slab), BF16),
        pltpu.VMEM((ny, tokens, slab), BF16),
        pltpu.VMEM((ny, 2, tokens, states), BF16), pltpu.VMEM((ny, 2, tokens, states), BF16),
        pltpu.VMEM((nz, tokens, 2 * LANE), BF16), pltpu.VMEM((nz, tokens, 2 * LANE), BF16),
        pltpu.VMEM((2 * LANE, nz * tokens), BF16),
        pltpu.VMEM((ny, nx, 2 * LANE, LANE), F32),
        pltpu.VMEM((nx, ny, 2 * LANE, LANE), BF16), pltpu.VMEM((nx, ny, 2 * LANE, LANE), BF16),
        pltpu.VMEM((ny, 2 * LANE, LANE), BF16), pltpu.VMEM((ny, 2 * LANE, LANE), BF16),
        pltpu.VMEM((nz, rows_z, 2 * LANE), F32), pltpu.VMEM((nz, rows_z, 2 * LANE), F32),
        pltpu.VMEM((nz, 1, line), F32), pltpu.VMEM((nx, 1, line), F32),
        pltpu.VMEM((nz, 1, 9 * states), F32), pltpu.VMEM((nx, 1, 9 * states), F32),
        pltpu.VMEM((ny, 1, 3 * states), F32),
        dma((3,)), dma, dma((ny,)), dma((stages,)), dma((stages, 2, nz)), dma((stages,)), dma((stages,)),
        *[dma for _ in range(10)],
        *[dma for _ in range(10)],
    ]
    vmem = pl.BlockSpec(memory_space=pltpu.VMEM)
    smem = pl.BlockSpec(memory_space=pltpu.SMEM)
    hbm = pl.BlockSpec(memory_space=pl.ANY)
    results = pl.pallas_call(
        functools.partial(kernel, dims),
        out_shape=(
            jax.ShapeDtypeStruct((tokens, 2, states), BF16),
            jax.ShapeDtypeStruct((rows_z, 2, states), F32),
            jax.ShapeDtypeStruct((2, states), F32),
            jax.ShapeDtypeStruct((1, states), F32),
        ),
        in_specs=[smem, vmem, vmem, vmem, vmem, vmem, hbm, hbm, hbm],
        out_specs=(hbm, vmem, vmem, vmem),
        scratch_shapes=scratch,
        compiler_params=pltpu.CompilerParams(
            collective_id=0, has_side_effects=True, vmem_limit_bytes=56 * 1024 * 1024
        ),
    )(
        doc_starts, row_blocks[None], modulus[None], phase[None], gain[None], retain,
        inputs[0], cotangent[0], out_proj,
    )
    grad_inputs, grad_proj, grad_eigen, grad_gain = pl.pallas_call(
        hand_over,
        out_shape=tuple(jax.ShapeDtypeStruct(r.shape, r.dtype) for r in results),
        in_specs=[vmem] * 4,
        out_specs=(vmem,) * 4,
    )(*results)
    return grad_inputs[None], grad_proj, grad_eigen, grad_gain[0]


def solution(mesh):
    sizes = mesh.shape
    nx, nz = grid_of(sizes["ctx"])
    dims = (sizes["dp"], nx, nz, sizes["chan"])
    return jax.shard_map(
        functools.partial(body, dims),
        mesh=mesh,
        in_specs=(
            P("dp", "ctx", None, "chan"),
            P("dp", "ctx", None),
            P("dp", None, "chan"),
            P("chan"),
            P("chan"),
            P("chan"),
            P("dp", "ctx"),
            P("dp", None),
            P("dp"),
        ),
        out_specs=(
            P("dp", "ctx", None, "chan"),
            P(("dp", "ctx"), None, "chan"),
            P(None, "chan"),
            P("chan"),
        ),
        check_vma=False,
    )
```
